128 devices in a mesh: rows: 16 (over y, x), cols: 8 (over z, core).
Axes of the slice: x: 4, y: 4, z: 4, core: 2. Of those that a mesh axis runs over, the one named last changes fastest.
Arguments:
- node_features: float32 [98304, 256], P(('rows', 'cols')), may hold values from -24 to 24
- cotangent: float32 [98304, 256], P(('rows', 'cols')), may hold values from -6 to 6
- w_query: float32 [256, 256], replicated, may hold values from -0.375 to 0.375
- w_key: float32 [256, 256], replicated, may hold values from -0.375 to 0.375
- w_value: float32 [256, 256], replicated, may hold values from -0.375 to 0.375
- w_graph: float32 [256, 256], replicated, may hold values from -0.375 to 0.375
- tile_values: float32 [36864, 128, 128], P(('rows', 'cols')), may hold values from -0.078125 to 0.078125
- tile_rows: int32 [36864], P(('rows', 'cols')), may hold values from 0 to 47, as said below
- tile_cols: int32 [36864], P(('rows', 'cols')), may hold values from 0 to 95
- tile_count: int32 [128], P(('rows', 'cols')), may hold values from 36 to 288, as said below
Outputs:
- output: float32 [98304, 256], P(('rows', 'cols'))
- grad_x: float32 [98304, 256], P(('rows', 'cols'))
- grad_query: float32 [256, 256], replicated
- grad_key: float32 [256, 256], replicated
- grad_value: float32 [256, 256], replicated
- grad_graph: float32 [256, 256], replicated
The draws below stay inside these ranges and needn't reach their ends.
Inputs may be any that keep to these rules, and one draw needn't show every extreme that they name: The (tile_rows, tile_cols) pairs of one device's 288 slots are all different; slots past a device's count hold data that is not part of A. `tile_count`: some device has all 288 slots live and some device only 36.
All inputs are finite; a program needn't handle non-finite values.
Results may differ from the reference program's by a relative error of at most 0.0003.
Values sent between devices are 32-bit elements; how exact they have to be, the bound alone decides.
A program may use at most 192 MiB of HBM per device.

```python
import math
import jax
import jax.numpy as jnp
from jax import lax

D = 256
TILE = 128
NODE_DEV = 768
MAXT = 288
NODES = 98304
TILES = 36864
ROW_BLOCKS = 48
COL_BLOCKS = 96
N_ROWS = 16
N_COLS = 8


def draw_node_features(key, part):
    k_scale, k_offset, k_base = jax.random.split(key, 3)
    rise = 1.0 + 2.0 * jnp.arange(NODES, dtype=jnp.float32)[:, None] / (NODES - 1)
    row_scale = jnp.exp(jax.random.uniform(k_scale, (NODES, 1), jnp.float32, 0.0, math.log(4.0)))
    offsets = jnp.clip(jax.random.normal(k_offset, (NODES // NODE_DEV, D), jnp.float32), -3.0, 3.0)
    offsets = jnp.repeat(offsets, NODE_DEV, axis=0)
    base = jnp.clip(jax.random.normal(k_base, (NODES, D), jnp.float32), -4.0, 4.0)
    result = rise * (0.35 * row_scale * base + 0.6 * offsets)
    return result.astype(jnp.float32)


def tile_positions(key):
    device_keys = jax.random.split(jax.random.fold_in(key, 11), TILES // MAXT)

    def one_device(device_key):
        return jax.random.permutation(device_key, ROW_BLOCKS * COL_BLOCKS)[:MAXT]
    return jax.vmap(one_device)(device_keys).reshape(-1).astype(jnp.int32)


def draw_tile_rows(key, part):
    return (tile_positions(key) // COL_BLOCKS).astype(jnp.int32)


def draw_tile_cols(key, part):
    return (tile_positions(key) % COL_BLOCKS).astype(jnp.int32)


def draw_tile_count(key, part):
    devices = TILES // MAXT
    k_shift, k_order = jax.random.split(jax.random.fold_in(key, 23))
    shifts = jax.random.randint(k_shift, (devices,), 0, 4)
    counts = MAXT // jnp.left_shift(jnp.ones((devices,), jnp.int32), shifts)
    order = jax.random.permutation(k_order, devices)
    counts = counts.at[order[0]].set(MAXT).at[order[1]].set(MAXT // 8)
    return counts.astype(jnp.int32)


def steps_of(key, shape, pieces, smallest, top_value):
    factor_of, own = 1.0, jax.random.fold_in(key, 6)
    for dim, parts in pieces:
        steps = jnp.exp(jax.random.uniform(jax.random.fold_in(own, dim), (parts,), jnp.float32, smallest / len(pieces), top_value / len(pieces)))
        factor_of = factor_of * jnp.repeat(steps, shape[dim] // parts).reshape([-1 if axis == dim else 1 for axis in range(len(shape))])
    return factor_of


def noise(stream_key, extent, scale, reach, shards=(), held_as=jnp.bfloat16):
    values = jax.random.normal(stream_key, extent, jnp.float32) * scale
    if len(shards) > 0:
        values = steps_of(stream_key, extent, shards, -0.22, 0.18) * values
    return jnp.clip(values, min=-reach, max=reach).astype(held_as)


def setup_inputs(seed: int = 0) -> dict:
    key_of = jax.random.split(jax.random.key(seed), 11)
    return {
        "node_features": draw_node_features(jax.random.fold_in(key_of[10], 71), 0),
        "cotangent": noise(key_of[1], (NODES, D), 1.0, 6.0, ((0, 128),), jnp.float32),
        "w_query": noise(key_of[2], (D, D), D ** -0.5, 0.375, (), jnp.float32),
        "w_key": noise(key_of[3], (D, D), D ** -0.5, 0.375, (), jnp.float32),
        "w_value": noise(key_of[4], (D, D), D ** -0.5, 0.375, (), jnp.float32),
        "w_graph": noise(key_of[5], (D, D), D ** -0.5, 0.375, (), jnp.float32),
        "tile_values": noise(key_of[6], (TILES, TILE, TILE), (MAXT * TILE * TILE // NODE_DEV) ** -0.5, 0.078125, ((0, 128),), jnp.float32),
        "tile_rows": draw_tile_rows(jax.random.fold_in(key_of[10], 71), 0),
        "tile_cols": draw_tile_cols(jax.random.fold_in(key_of[10], 71), 0),
        "tile_count": draw_tile_count(jax.random.fold_in(key_of[10], 71), 0),
    }


def hi_dot(left, right):
    return jnp.dot(left, right, precision=lax.Precision.HIGHEST)


def elu_slope(inputs):
    return jnp.where(inputs > 0, 1.0, jnp.exp(jnp.minimum(inputs, 0.0)))


def aggregate(source, tile_values, tile_rows, tile_cols, tile_count):
    devices = N_ROWS * N_COLS
    group = NODE_DEV * N_COLS
    width = source.shape[1]
    layered = source.reshape(N_ROWS, N_COLS, NODE_DEV, width)
    all_values = tile_values.reshape(devices, MAXT, TILE, TILE)
    row_ids = tile_rows.reshape(devices, MAXT)
    col_ids = tile_cols.reshape(devices, MAXT)
    slot_ids = jnp.arange(MAXT, dtype=jnp.int32)

    def one_device(result, device):
        row_group = device // N_COLS
        column = device % N_COLS
        panel = lax.dynamic_index_in_dim(layered, column, 1, False).reshape(COL_BLOCKS, TILE, width)
        alive = (slot_ids < tile_count[device]).astype(source.dtype)
        block_values = all_values[device] * alive[:, None, None]
        picked = panel[col_ids[device]]
        product = jnp.einsum('tij,tjd->tid', block_values, picked, precision=lax.Precision.HIGHEST)
        placed = jnp.zeros((ROW_BLOCKS, TILE, width), source.dtype).at[row_ids[device]].add(product)
        result = result.at[row_group].add(placed.reshape(group, width))
        return result, None

    start = jnp.zeros((N_ROWS, group, width), source.dtype)
    result, _ = lax.scan(one_device, start, jnp.arange(devices, dtype=jnp.int32))
    return result.reshape(-1, width)


def aggregate_transpose(source, tile_values, tile_rows, tile_cols, tile_count):
    devices = N_ROWS * N_COLS
    group = NODE_DEV * N_COLS
    width = source.shape[1]
    layered = source.reshape(N_ROWS, group, width)
    all_values = tile_values.reshape(devices, MAXT, TILE, TILE)
    row_ids = tile_rows.reshape(devices, MAXT)
    col_ids = tile_cols.reshape(devices, MAXT)
    slot_ids = jnp.arange(MAXT, dtype=jnp.int32)

    def one_device(result, device):
        row_group = device // N_COLS
        column = device % N_COLS
        group_rows = lax.dynamic_index_in_dim(layered, row_group, 0, False).reshape(ROW_BLOCKS, TILE, width)
        alive = (slot_ids < tile_count[device]).astype(source.dtype)
        block_values = all_values[device] * alive[:, None, None]
        picked = group_rows[row_ids[device]]
        product = jnp.einsum('tji,tjd->tid', block_values, picked, precision=lax.Precision.HIGHEST)
        placed = jnp.zeros((COL_BLOCKS, TILE, width), source.dtype).at[col_ids[device]].add(product)
        result = result.at[:, column].add(placed.reshape(N_ROWS, NODE_DEV, width))
        return result, None

    start = jnp.zeros((N_ROWS, N_COLS, NODE_DEV, width), source.dtype)
    result, _ = lax.scan(one_device, start, jnp.arange(devices, dtype=jnp.int32))
    return result.reshape(-1, width)


def reference(node_features, cotangent, w_query, w_key, w_value, w_graph, tile_values, tile_rows, tile_cols, tile_count):
    query = hi_dot(node_features, w_query)
    key_proj = hi_dot(node_features, w_key)
    value_proj = hi_dot(node_features, w_value)
    feat_q = jax.nn.elu(query) + 1.0
    feat_k = jax.nn.elu(key_proj) + 1.0
    state = hi_dot(feat_k.T, value_proj)
    key_sum = jnp.sum(feat_k, axis=0)
    denominator = hi_dot(feat_q, key_sum)
    attended = hi_dot(feat_q, state) / denominator[:, None]
    projected = hi_dot(node_features, w_graph)
    graph_out = aggregate(projected, tile_values, tile_rows, tile_cols, tile_count)
    output = attended + graph_out

    scaled = cotangent / denominator[:, None]
    weight_dot = jnp.sum(cotangent * attended, axis=1) / denominator
    grad_feat_q = hi_dot(scaled, state.T) - weight_dot[:, None] * key_sum[None, :]
    grad_state = hi_dot(feat_q.T, scaled)
    grad_key_sum = -hi_dot(weight_dot, feat_q)
    grad_feat_k = hi_dot(value_proj, grad_state.T) + grad_key_sum[None, :]
    grad_values = hi_dot(feat_k, grad_state)
    grad_query_proj = grad_feat_q * elu_slope(query)
    grad_keys = grad_feat_k * elu_slope(key_proj)
    grad_projected = aggregate_transpose(cotangent, tile_values, tile_rows, tile_cols, tile_count)
    grad_query = hi_dot(node_features.T, grad_query_proj)
    grad_key = hi_dot(node_features.T, grad_keys)
    grad_value = hi_dot(node_features.T, grad_values)
    grad_graph = hi_dot(node_features.T, grad_projected)
    grad_x = hi_dot(grad_query_proj, w_query.T) + hi_dot(grad_keys, w_key.T)
    grad_x = grad_x + hi_dot(grad_values, w_value.T) + hi_dot(grad_projected, w_graph.T)
    return (output, grad_x, grad_query, grad_key, grad_value, grad_graph)
```

```python
import jax
import jax.numpy as jnp
from jax import lax
from jax.experimental import pallas as pl
from jax.experimental.pallas import tpu as pltpu
from jax.sharding import PartitionSpec as P

MESH = pl.DeviceIdType.MESH
F32, BF16 = jnp.float32, jnp.bfloat16
TILE, D, NODE, MAXT = 128, 256, 768, 288
HALF, QUART = NODE // 2, NODE // 4
BLK = NODE // TILE
CH = 256
NN, NT, TN = ((1,), (0,)), ((1,), (1,)), ((0,), (0,))


def dot(a, b, dims=NN):
    return lax.dot_general(
        a, b, (dims, ((), ())), precision=lax.Precision.HIGHEST, preferred_element_type=F32
    )


def feat(v):
    return jnp.where(v > 0, v + 1.0, jnp.exp(jnp.minimum(v, 0.0)))


def slope(v):
    return jnp.where(v > 0, 1.0, jnp.exp(jnp.minimum(v, 0.0)))


def split2(v):
    hi = v.astype(BF16)
    return hi, (v - hi.astype(F32)).astype(BF16)


class Net:
    def __init__(self, ssem, rsem):
        self.ssem, self.rsem, self.n, self.sent = ssem, rsem, 0, []
        self.r, self.c = lax.axis_index("rows"), lax.axis_index("cols")
        self.y, self.x = self.r // 4, self.r % 4
        self.z, self.k = self.c // 2, self.c % 2

    def send(self, src, dst, row=None, col=None):
        i, self.n = self.n, self.n + 1
        copy = pltpu.make_async_remote_copy(
            src_ref=src,
            dst_ref=dst,
            send_sem=self.ssem.at[i],
            recv_sem=self.rsem.at[i],
            device_id=(self.r if row is None else row, self.c if col is None else col),
            device_id_type=MESH,
        )
        copy.start()
        self.sent.append(copy)
        return copy

    def barrier(self):
        sem = pltpu.get_barrier_semaphore()
        there = [(self.r, (self.c + j) % 8) for j in range(1, 8)]
        there += [(self.y * 4 + (self.x + j) % 4, self.c) for j in range(1, 4)]
        there += [((self.y + j) % 4 * 4 + self.x, self.c) for j in range(1, 4)]
        for device in there:
            pl.semaphore_signal(sem, inc=1, device_id=device, device_id_type=MESH)
        pl.semaphore_wait(sem, len(there))

    def finish(self):
        for copy in self.sent:
            copy.wait_send()


def all_reduce(net, part, r1, red1, r2, red2, r3, full1, full):
    r, c, x, y = net.r, net.c, net.x, net.y
    first = []
    for j in range(1, 8):
        to = (c + j) % 8
        first.append(net.send(part.at[pl.ds(to * 4, 4)], r1.at[j - 1], col=to))
    yield
    for copy in first:
        copy.wait_recv()
    total = part[pl.ds(c * 4, 4)]
    for j in range(7):
        total = total + r1[j]
    red1[...] = total
    second = []
    for j in range(1, 4):
        to = (x + j) % 4
        second.append(net.send(red1.at[to], r2.at[j - 1], row=y * 4 + to))
    yield
    for copy in second:
        copy.wait_recv()
    r3[pl.ds(y, 1)] = (red1[pl.ds(x, 1)] + r2[0:1]) + (r2[1:2] + r2[2:3])
    third = [
        net.send(r3.at[y], r3.at[y], row=(y + j) % 4 * 4 + x) for j in range(1, 4)
    ]
    yield
    for copy in third:
        copy.wait_recv()
    full1[pl.ds(x, 1)] = (r3[0:1] + r3[1:2]) + (r3[2:3] + r3[3:4])
    fourth = [
        net.send(full1.at[x], full1.at[x], row=y * 4 + (x + j) % 4) for j in range(1, 4)
    ]
    yield
    for copy in fourth:
        copy.wait_recv()
    full[pl.ds(c * 4, 4)] = full1[...]
    fifth = [
        net.send(full1, full.at[pl.ds(c * 4, 4)], col=(c + j) % 8) for j in range(1, 8)
    ]
    yield
    for copy in fifth:
        copy.wait_recv()


def reduce_scratch(n):
    return [
        pltpu.VMEM((32, n, D), F32),
        pltpu.VMEM((7, 4, n, D), F32),
        pltpu.VMEM((4, n, D), F32),
        pltpu.VMEM((3, n, D), F32),
        pltpu.VMEM((n, D), F32),
        pltpu.VMEM((4, n, D), F32),
        pltpu.VMEM((4, n, D), F32),
        pltpu.VMEM((32, n, D), F32),
    ]


REDUCE_COPIES = 7 + 3 + 3 + 3 + 7


def row_order(net, base):
    if base == 0:
        return net.x, net.y, lambda first, then: then % 4 * 4 + first % 4
    return net.y, net.x, lambda first, then: first % 4 * 4 + then % 4


def gather_half(net, mine, panel, base, done):
    a, b, slot = row_order(net, base)
    all_rows, up, down = pl.ds(base, HALF), pl.ds(base, QUART), pl.ds(base + QUART, QUART)

    def pair(src, at, rows, plus, minus):
        view = panel.at[at, rows]
        source = view if src is None else src.at[rows]
        return net.send(source, view, row=plus), net.send(source, view, row=minus)

    def forward(at, rows, row):
        return net.send(panel.at[at, rows], panel.at[at, rows], row=row)

    own = slot(a, b)
    a_plus, a_minus = slot(a + 1, b), slot(a - 1 + 4, b)
    b_plus, b_minus = slot(a, b + 1), slot(a, b - 1 + 4)
    from_left, from_right = pair(mine, own, all_rows, a_plus, a_minus)
    second = {0: pair(mine, own, all_rows, b_plus, b_minus)}
    yield
    from_left.wait_recv()
    fwd_up = forward(slot(a + 3, b), up, a_plus)
    second[3] = pair(None, slot(a + 3, b), all_rows, b_plus, b_minus)
    from_right.wait_recv()
    fwd_down = forward(slot(a + 1, b), down, a_minus)
    second[1] = pair(None, slot(a + 1, b), all_rows, b_plus, b_minus)
    done(3, 0)
    done(1, 0)
    third = {}

    def pass_on(o):
        left, right = second[o]
        left.wait_recv()
        f_up = forward(slot(a + o, b + 3), up, b_plus)
        right.wait_recv()
        f_down = forward(slot(a + o, b + 1), down, b_minus)
        third[o] = (f_up, f_down)
        done(o, 3)
        done(o, 1)

    yield
    pass_on(0)
    yield
    fwd_up.wait_recv()
    fwd_down.wait_recv()
    second[2] = pair(None, slot(a + 2, b), all_rows, b_plus, b_minus)
    done(2, 0)
    yield
    pass_on(3)
    yield
    pass_on(1)
    yield
    for copy in third[0]:
        copy.wait_recv()
    done(0, 2)
    yield
    pass_on(2)
    yield
    for o in (3, 1, 2):
        for copy in third[o]:
            copy.wait_recv()
        done(o, 2)
        yield


GATHER_COPIES = 2 + 2 + 4 * 4


def gather_cols(net, mine, panel, done):
    z, k = net.z, net.k
    own = net.c
    plus, minus = (z + 1) % 4 * 2 + k, (z + 3) % 4 * 2 + k
    opposite = (z + 2) % 4 * 2 + k
    sibling = z * 2 + 1 - k
    up, down = pl.ds(0, HALF), pl.ds(HALF, HALF)
    left = net.send(mine, panel.at[own], col=plus)
    right = net.send(mine, panel.at[own], col=minus)
    pair = [net.send(mine, panel.at[own], col=sibling)]
    yield
    left.wait_recv()
    f_up = net.send(panel.at[minus, up], panel.at[minus, up], col=plus)
    pair.append(net.send(panel.at[minus], panel.at[minus], col=sibling))
    right.wait_recv()
    f_down = net.send(panel.at[plus, down], panel.at[plus, down], col=minus)
    pair.append(net.send(panel.at[plus], panel.at[plus], col=sibling))
    done(minus)
    done(plus)
    yield
    f_up.wait_recv()
    f_down.wait_recv()
    pair.append(net.send(panel.at[opposite], panel.at[opposite], col=sibling))
    done(opposite)
    yield
    for o, copy in zip((0, 3, 1, 2), pair):
        copy.wait_recv()
        done((z + o) % 4 * 2 + 1 - k)
    yield


COLS_COPIES = 3 + 4 + 1


def drive(*runs):
    runs = list(runs)
    while runs:
        for run in list(runs):
            try:
                next(run)
            except StopIteration:
                runs.remove(run)


def gather_kernel(
    x_ref, c_ref, wq_ref, wk_ref, wv_ref,
    xs_ref, cs_ref, att_ref, gq_ref, key_ref, val_ref, gs_ref, gks_ref,
    q_ref, xp, cp, x_stage, c_stage, stage_sem, ssem, rsem, *reduce_refs,
):
    net = Net(ssem, rsem)
    net.barrier()
    ar1, ar2 = reduce_refs[:8], reduce_refs[8:]
    staged = []

    def split_out(source, stage, out, slot):
        @pl.loop(0, BLK)
        def _(i):
            hi, lo = split2(source[pl.ds(pl.multiple_of(i * TILE, TILE), TILE), :])
            stage[slot, i, 0:TILE, :] = hi
            stage[slot, i, TILE : 2 * TILE, :] = lo

        copy = pltpu.make_async_copy(stage.at[slot], out.at[slot], stage_sem.at[len(staged)])
        copy.start()
        staged.append(copy)

    seen = set()

    def x_done(dx, dy):
        if (dx, dy) in seen:
            slot = (net.y + dy) % 4 * 4 + (net.x + dx) % 4
            split_out(xp.at[slot], x_stage, xs_ref, slot)
        seen.add((dx, dy))

    def cols_done(slot):
        split_out(cp.at[slot], c_stage, cs_ref, slot)

    def attention():
        part, full = ar1[0], ar1[7]
        part2, full2 = ar2[0], ar2[7]

        def first(i, sums):
            state, key_sum = sums
            rows = pl.ds(pl.multiple_of(i * CH, CH), CH)
            x = x_ref[rows, :]
            q_ref[rows, :] = dot(x, wq_ref[...])
            key = dot(x, wk_ref[...])
            val = dot(x, wv_ref[...])
            key_ref[rows, :] = key
            val_ref[rows, :] = val
            feat_k = feat(key)
            return state + dot(feat_k, val, TN), key_sum + jnp.sum(feat_k, axis=0, keepdims=True)

        zero = (jnp.zeros((D, D), F32), jnp.zeros((1, D), F32))
        state, key_sum = lax.fori_loop(0, NODE // CH, first, zero)
        part[:, 0:8, :] = state.reshape(32, 8, D)
        part[:, 8:16, :] = jnp.broadcast_to(key_sum[None], (32, 8, D))
        yield from all_reduce(net, *ar1)
        state_ref, key_row = full, full[0, 8:9, :]
        state = state_ref[:, 0:8, :].reshape(D, D)

        def second(i, sums):
            grad_state, grad_key_sum = sums
            rows = pl.ds(pl.multiple_of(i * CH, CH), CH)
            q = q_ref[rows, :]
            cot = c_ref[rows, :]
            feat_q = feat(q)
            den = jnp.sum(feat_q * key_row, axis=1, keepdims=True)
            att = dot(feat_q, state) / den
            att_ref[rows, :] = att
            scaled = cot / den
            weight_dot = jnp.sum(cot * att, axis=1, keepdims=True) / den
            gq_ref[rows, :] = (dot(scaled, state, NT) - weight_dot * key_row) * slope(q)
            return (
                grad_state + dot(feat_q, scaled, TN),
                grad_key_sum - jnp.sum(feat_q * weight_dot, axis=0, keepdims=True),
            )

        grad_state, grad_key_sum = lax.fori_loop(0, NODE // CH, second, zero)
        part2[:, 0:8, :] = grad_state.reshape(32, 8, D)
        part2[:, 8:16, :] = jnp.broadcast_to(grad_key_sum[None], (32, 8, D))
        yield from all_reduce(net, *ar2)
        gs_ref[...] = full2[:, 0:8, :].reshape(D, D)
        gks_ref[...] = full2[0, 8:16, :]

    def own_blocks():
        yield
        split_out(x_ref, x_stage, xs_ref, net.r)
        split_out(c_ref, c_stage, cs_ref, net.c)

    drive(
        gather_half(net, x_ref, xp, 0, x_done),
        gather_half(net, x_ref, xp, HALF, lambda dy, dx: x_done(dx, dy)),
        gather_cols(net, c_ref, cp, cols_done),
        attention(),
        own_blocks(),
    )
    net.finish()
    for copy in staged:
        copy.wait()


def run_gather(x, cot, wq, wk, wv):
    copies = 2 * GATHER_COPIES + COLS_COPIES + 2 * REDUCE_COPIES
    block = jax.ShapeDtypeStruct((NODE, D), F32)
    vmem, hbm = pl.BlockSpec(memory_space=pltpu.VMEM), pl.BlockSpec(memory_space=pl.ANY)
    return pl.pallas_call(
        gather_kernel,
        out_shape=[
            jax.ShapeDtypeStruct((16, BLK, 2 * TILE, D), BF16),
            jax.ShapeDtypeStruct((8, BLK, 2 * TILE, D), BF16),
            block, block, block, block,
            jax.ShapeDtypeStruct((D, D), F32),
            jax.ShapeDtypeStruct((8, D), F32),
        ],
        in_specs=[vmem] * 5,
        out_specs=[hbm, hbm] + [vmem] * 6,
        scratch_shapes=[
            pltpu.VMEM((NODE, D), F32),
            pltpu.VMEM((16, NODE, D), F32),
            pltpu.VMEM((8, NODE, D), F32),
            pltpu.VMEM((16, BLK, 2 * TILE, D), BF16),
            pltpu.VMEM((8, BLK, 2 * TILE, D), BF16),
            pltpu.SemaphoreType.DMA((24,)),
            pltpu.SemaphoreType.DMA((copies,)),
            pltpu.SemaphoreType.DMA((copies,)),
        ]
        + reduce_scratch(16)
        + reduce_scratch(16),
        compiler_params=pltpu.CompilerParams(
            collective_id=0, has_side_effects=True, vmem_limit_bytes=60 * 2**20
        ),
        name="gather",
    )(x, cot, wq, wk, wv)


CHUNK = 16
SLOTS = 3
GROUP = 4


def tile_kernel(
    rows_ref, cols_ref, count_ref, tiles_ref, xs_ref, cs_ref,
    f_ref, t_ref,
    xs, cs, f, t, buf, sem, tile_sem,
):
    count = count_ref[0]
    chunks = (count + CHUNK - 1) // CHUNK
    load_c = pltpu.make_async_copy(cs_ref, cs, sem.at[0])
    load_x = pltpu.make_async_copy(xs_ref, xs, sem.at[1])

    def fetch(chunk, slot):
        return pltpu.make_async_copy(
            tiles_ref.at[pl.ds(chunk * CHUNK, CHUNK)], buf.at[slot], tile_sem.at[slot]
        )

    def sweep(body):
        for i in range(SLOTS - 1):
            @pl.when(i < chunks)
            def _(i=i):
                fetch(i, i).start()

        @pl.loop(0, chunks)
        def _(chunk):
            slot = chunk % SLOTS

            @pl.when(chunk + SLOTS - 1 < chunks)
            def _():
                fetch(chunk + SLOTS - 1, (chunk + SLOTS - 1) % SLOTS).start()

            fetch(chunk, slot).wait()

            @pl.loop(0, CHUNK // GROUP)
            def _(group):
                first = group * GROUP
                for i in range(GROUP):
                    at = chunk * CHUNK + first + i
                    tile = buf[slot, first + i]
                    body(jnp.where(at < count, tile, 0.0), rows_ref[at], cols_ref[at])

    def product(tile, panel):
        hi, lo = split2(tile)
        left = jnp.concatenate(
            [jnp.concatenate([hi, hi], axis=1), jnp.concatenate([lo, lo], axis=1)], axis=0
        )
        both = jnp.dot(left, panel, preferred_element_type=F32)
        return both[0:TILE] + both[TILE : 2 * TILE]

    def backward(tile, row, col):
        t[col] += product(tile.T, cs[row])

    def forward(tile, row, col):
        f[row] += product(tile, xs[col])

    load_c.start()
    load_x.start()
    t[...] = jnp.zeros_like(t)
    f[...] = jnp.zeros_like(f)
    load_c.wait()
    sweep(backward)
    store_t = pltpu.make_async_copy(t, t_ref, sem.at[2])
    store_t.start()
    load_x.wait()
    sweep(forward)
    store_f = pltpu.make_async_copy(f, f_ref, sem.at[3])
    store_f.start()
    store_t.wait()
    store_f.wait()


def run_tiles(tile_rows, tile_cols, tile_count, tiles, xs, cs):
    hbm, smem = pl.BlockSpec(memory_space=pl.ANY), pl.BlockSpec(memory_space=pltpu.SMEM)
    return pl.pallas_call(
        tile_kernel,
        out_shape=[
            jax.ShapeDtypeStruct((8 * BLK, TILE, D), F32),
            jax.ShapeDtypeStruct((16 * BLK, TILE, D), F32),
        ],
        in_specs=[smem] * 3 + [hbm] * 3,
        out_specs=[hbm] * 2,
        scratch_shapes=[
            pltpu.VMEM((16 * BLK, 2 * TILE, D), BF16),
            pltpu.VMEM((8 * BLK, 2 * TILE, D), BF16),
            pltpu.VMEM((8 * BLK, TILE, D), F32),
            pltpu.VMEM((16 * BLK, TILE, D), F32),
            pltpu.VMEM((SLOTS, CHUNK, TILE, TILE), F32),
            pltpu.SemaphoreType.DMA((4,)),
            pltpu.SemaphoreType.DMA((SLOTS,)),
        ],
        compiler_params=pltpu.CompilerParams(vmem_limit_bytes=60 * 2**20),
        name="tiles",
    )(
        tile_rows, tile_cols, tile_count, tiles,
        xs.reshape(16 * BLK, 2 * TILE, D), cs.reshape(8 * BLK, 2 * TILE, D),
    )


def scatter_half(net, t_hbm, t, base, leaf, main, leaf2, main2, ready):
    s, b, slot = row_order(net, base)
    up, down, both = pl.ds(base, QUART), pl.ds(base + QUART, QUART), pl.ds(base, HALF)
    order = (2, 1, 3, 0)
    b_plus, b_minus = slot(s, b + 1), slot(s, b + 3)
    leaves, mains = [], []
    for i, o in enumerate(order):
        at = slot(s + o, b + 2)
        leaves.append(
            (
                net.send(t_hbm.at[at, up], leaf.at[i, 0], row=b_plus),
                net.send(t_hbm.at[at, down], leaf.at[i, 1], row=b_minus),
            )
        )
    yield
    ready()
    for i, o in enumerate(order):
        for copy in leaves[i]:
            copy.wait_recv()
        plus, minus = slot(s + o, b + 1), slot(s + o, b + 3)
        t[plus, up] += leaf[i, 0]
        t[minus, down] += leaf[i, 1]
        mains.append(
            (
                net.send(t.at[plus, both], main.at[i, 0], row=b_plus),
                net.send(t.at[minus, both], main.at[i, 1], row=b_minus),
            )
        )
        yield
    s_plus, s_minus = slot(s + 1, b), slot(s + 3, b)
    for i, o in enumerate(order):
        for copy in mains[i]:
            copy.wait_recv()
        at = slot(s + o, b)
        t[at, both] += main[i, 0] + main[i, 1]
        if o == 2:
            leaves2 = (
                net.send(t.at[at, up], leaf2.at[0], row=s_plus),
                net.send(t.at[at, down], leaf2.at[1], row=s_minus),
            )
        if o == 3:
            for copy in leaves2:
                copy.wait_recv()
            t[s_plus, up] += leaf2[0]
            t[s_minus, down] += leaf2[1]
            mains2 = (
                net.send(t.at[s_plus, both], main2.at[0], row=s_plus),
                net.send(t.at[s_minus, both], main2.at[1], row=s_minus),
            )
        yield
    for copy in mains2:
        copy.wait_recv()
    t[slot(s, b), both] += main2[0] + main2[1]


SCATTER_COPIES = GATHER_COPIES


def scatter_cols(net, f_hbm, f, pair, leaf, main, ready):
    z, k = net.z, net.k
    up, down = pl.ds(0, HALF), pl.ds(HALF, HALF)
    order = (2, 1, 3, 0)
    copies = [
        net.send(f_hbm.at[(z + o) % 4 * 2 + 1 - k], pair.at[i], col=z * 2 + 1 - k)
        for i, o in enumerate(order)
    ]
    yield
    ready()
    plus, minus = (z + 1) % 4 * 2 + k, (z + 3) % 4 * 2 + k
    for i, o in enumerate(order):
        copies[i].wait_recv()
        at = (z + o) % 4 * 2 + k
        f[at] += pair[i]
        if o == 2:
            leaves = (
                net.send(f.at[at, up], leaf.at[0], col=plus),
                net.send(f.at[at, down], leaf.at[1], col=minus),
            )
            yield
    yield
    for copy in leaves:
        copy.wait_recv()
    f[plus, up] += leaf[0]
    f[minus, down] += leaf[1]
    mains = (
        net.send(f.at[plus], main.at[0], col=plus),
        net.send(f.at[minus], main.at[1], col=minus),
    )
    yield
    for copy in mains:
        copy.wait_recv()
    f[net.c] += main[0] + main[1]


SCATTER_COLS_COPIES = 4 + 2 + 2


def scatter_kernel(
    x_ref, c_ref, wq_ref, wk_ref, wv_ref, wg_ref,
    att_ref, gq_ref, key_ref, val_ref, gs_ref, gks_ref, f_hbm, t_hbm,
    out_ref, gx_ref, dq_ref, dk_ref, dv_ref, dg_ref,
    f, t, leaf, main, leaf2, main2, pair, zleaf, zmain, load_sem, ssem, rsem, *reduce_refs,
):
    net = Net(ssem, rsem)
    load_t = pltpu.make_async_copy(t_hbm, t, load_sem.at[0])
    load_f = pltpu.make_async_copy(f_hbm, f, load_sem.at[1])
    load_t.start()
    load_f.start()
    net.barrier()
    ar1, ar2 = reduce_refs[:8], reduce_refs[8:]

    def ready(copy):
        pending = [copy]

        def once():
            if pending:
                pending.pop().wait()

        return once

    def attention():
        part, full = ar1[0], ar1[7]
        zero = jnp.zeros((D, D), F32)

        dq_ref[...] = zero
        dk_ref[...] = zero
        dv_ref[...] = zero

        @pl.loop(0, NODE // CH)
        def _(i):
            rows = pl.ds(pl.multiple_of(i * CH, CH), CH)
            x = x_ref[rows, :]
            key = key_ref[rows, :]
            gq = gq_ref[rows, :]
            gk = (dot(val_ref[rows, :], gs_ref[...], NT) + gks_ref[0:1, :]) * slope(key)
            gv = dot(feat(key), gs_ref[...])
            gx = dot(gq, wq_ref[...], NT) + dot(gk, wk_ref[...], NT)
            gx_ref[rows, :] = gx + dot(gv, wv_ref[...], NT)
            dq_ref[...] += dot(x, gq, TN)
            dk_ref[...] += dot(x, gk, TN)
            dv_ref[...] += dot(x, gv, TN)

        for i, grad in enumerate((dq_ref, dk_ref, dv_ref)):
            part[:, 8 * i : 8 * i + 8, :] = grad[...].reshape(32, 8, D)
        yield from all_reduce(net, *ar1)
        for i, grad in enumerate((dq_ref, dk_ref, dv_ref)):
            grad[...] = full[:, 8 * i : 8 * i + 8, :].reshape(D, D)

    def graph():
        part, full = ar2[0], ar2[7]
        yield from scatter_cols(net, f_hbm, f, pair, zleaf, zmain, ready(load_f))
        dg_ref[...] = jnp.zeros((D, D), F32)

        @pl.loop(0, NODE // CH)
        def _(i):
            rows = pl.ds(pl.multiple_of(i * CH, CH), CH)
            mixed = f[net.c, rows, :]
            out_ref[rows, :] = att_ref[rows, :] + dot(mixed, wg_ref[...])
            dg_ref[...] += dot(mixed, c_ref[rows, :], TN)

        part[...] = dg_ref[...].reshape(32, 8, D)
        yield from all_reduce(net, *ar2)
        dg_ref[...] = full[...].reshape(D, D)

    once_t = ready(load_t)
    drive(
        scatter_half(net, t_hbm, t, 0, leaf.at[0], main.at[0], leaf2.at[0], main2.at[0], once_t),
        scatter_half(net, t_hbm, t, HALF, leaf.at[1], main.at[1], leaf2.at[1], main2.at[1], once_t),
        graph(),
        attention(),
    )

    @pl.loop(0, NODE // CH)
    def _(i):
        rows = pl.ds(pl.multiple_of(i * CH, CH), CH)
        gx_ref[rows, :] += dot(t[net.r, rows, :], wg_ref[...], NT)

    net.finish()


def run_scatter(x, cot, wq, wk, wv, wg, att, gq, key, val, gs, gks, f, t):
    copies = 2 * SCATTER_COPIES + SCATTER_COLS_COPIES + 2 * REDUCE_COPIES
    block, weight = jax.ShapeDtypeStruct((NODE, D), F32), jax.ShapeDtypeStruct((D, D), F32)
    vmem, hbm = pl.BlockSpec(memory_space=pltpu.VMEM), pl.BlockSpec(memory_space=pl.ANY)
    return pl.pallas_call(
        scatter_kernel,
        out_shape=[block, block, weight, weight, weight, weight],
        in_specs=[vmem] * 12 + [hbm] * 2,
        out_specs=[vmem] * 6,
        scratch_shapes=[
            pltpu.VMEM((8, NODE, D), F32),
            pltpu.VMEM((16, NODE, D), F32),
            pltpu.VMEM((2, 4, 2, QUART, D), F32),
            pltpu.VMEM((2, 4, 2, HALF, D), F32),
            pltpu.VMEM((2, 2, QUART, D), F32),
            pltpu.VMEM((2, 2, HALF, D), F32),
            pltpu.VMEM((4, NODE, D), F32),
            pltpu.VMEM((2, HALF, D), F32),
            pltpu.VMEM((2, NODE, D), F32),
            pltpu.SemaphoreType.DMA((2,)),
            pltpu.SemaphoreType.DMA((copies,)),
            pltpu.SemaphoreType.DMA((copies,)),
        ]
        + reduce_scratch(24)
        + reduce_scratch(8),
        compiler_params=pltpu.CompilerParams(
            collective_id=1, has_side_effects=True, vmem_limit_bytes=60 * 2**20
        ),
        name="scatter",
    )(x, cot, wq, wk, wv, wg, att, gq, key, val, gs, gks, f, t)


def per_device(x, cot, wq, wk, wv, wg, tiles, tile_rows, tile_cols, tile_count):
    xs, cs, att, gq, key, val, gs, gks = run_gather(x, cot, wq, wk, wv)
    f, t = run_tiles(tile_rows, tile_cols, tile_count, tiles, xs, cs)
    f, t = f.reshape(8, NODE, D), t.reshape(16, NODE, D)
    return tuple(run_scatter(x, cot, wq, wk, wv, wg, att, gq, key, val, gs, gks, f, t))


def solution(mesh):
    nodes = P(("rows", "cols"), None)
    slots = P(("rows", "cols"))
    return jax.shard_map(
        per_device,
        mesh=mesh,
        in_specs=(nodes, nodes, P(), P(), P(), P(), P(("rows", "cols"), None, None), slots, slots, slots),
        out_specs=(nodes, nodes, P(), P(), P(), P()),
        check_vma=False,
    )
```

```python
import jax
import jax.numpy as jnp
from jax import lax
from jax.experimental import pallas as pl
from jax.experimental.pallas import tpu as pltpu
from jax.sharding import PartitionSpec as P

MESH = pl.DeviceIdType.MESH
F32, BF16 = jnp.float32, jnp.bfloat16
TILE, D, NODE, MAXT = 128, 256, 768, 288
HALF, QUART = NODE // 2, NODE // 4
BLK = NODE // TILE
CH = 384
NN, NT, TN = ((1,), (0,)), ((1,), (1,)), ((0,), (0,))


def dot(a, b, dims=NN):
    (a_hi, a_lo), (b_hi, b_lo) = split2(a), split2(b)

    def one(p, q):
        return lax.dot_general(p, q, (dims, ((), ())), preferred_element_type=F32)

    return one(a_hi, b_hi) + (one(a_hi, b_lo) + one(a_lo, b_hi))


def feat(v):
    return jnp.where(v > 0, v + 1.0, jnp.exp(jnp.minimum(v, 0.0)))


def slope(v):
    return jnp.where(v > 0, 1.0, jnp.exp(jnp.minimum(v, 0.0)))


def split2(v):
    hi = v.astype(BF16)
    return hi, (v - hi.astype(F32)).astype(BF16)


class Net:
    def __init__(self, ssem, rsem):
        self.ssem, self.rsem, self.n, self.sent = ssem, rsem, 0, []
        self.r, self.c = lax.axis_index("rows"), lax.axis_index("cols")
        self.y, self.x = self.r // 4, self.r % 4
        self.z, self.k = self.c // 2, self.c % 2

    def send(self, src, dst, row=None, col=None):
        i, self.n = self.n, self.n + 1
        copy = pltpu.make_async_remote_copy(
            src_ref=src,
            dst_ref=dst,
            send_sem=self.ssem.at[i],
            recv_sem=self.rsem.at[i],
            device_id=(self.r if row is None else row, self.c if col is None else col),
            device_id_type=MESH,
        )
        copy.start()
        self.sent.append(copy)
        return copy

    def barrier(self):
        sem = pltpu.get_barrier_semaphore()
        there = [(self.r, (self.c + j) % 8) for j in range(1, 8)]
        there += [(self.y * 4 + (self.x + j) % 4, self.c) for j in range(1, 4)]
        there += [((self.y + j) % 4 * 4 + self.x, self.c) for j in range(1, 4)]
        for device in there:
            pl.semaphore_signal(sem, inc=1, device_id=device, device_id_type=MESH)
        pl.semaphore_wait(sem, len(there))

    def finish(self):
        for copy in self.sent:
            copy.wait_send()


def all_reduce(net, part, key, r1, kbuf, r2, r3, full):
    c, x, y = net.c, net.x, net.y
    n = part.shape[1]
    first = [net.send(part.at[(c + j) % 8], r1.at[j - 1], col=(c + j) % 8) for j in range(1, 8)]
    if key is not None:
        first += [net.send(key, kbuf.at[j - 1], col=(c + j) % 8) for j in range(1, 8)]
    yield
    for copy in first:
        copy.wait_recv()
    total = part[c]
    for j in range(7):
        total = total + r1[j]
    r2[x, 0:n] = total
    if key is not None:
        total = key[...]
        for j in range(7):
            total = total + kbuf[j]
        r2[x, n:] = total
    second = [net.send(r2.at[x], r2.at[x], row=y * 4 + (x + j) % 4) for j in range(1, 4)]
    yield
    for copy in second:
        copy.wait_recv()
    r3[y] = (r2[0] + r2[1]) + (r2[2] + r2[3])
    third = [net.send(r3.at[y], r3.at[y], row=(y + j) % 4 * 4 + x) for j in range(1, 4)]
    yield
    for copy in third:
        copy.wait_recv()
    full[c] = (r3[0, 0:n] + r3[1, 0:n]) + (r3[2, 0:n] + r3[3, 0:n])
    fourth = [net.send(full.at[c], full.at[c], col=(c + j) % 8) for j in range(1, 8)]
    yield
    for copy in fourth:
        copy.wait_recv()


def key_total(r3, n):
    return (r3[0, n:] + r3[1, n:]) + (r3[2, n:] + r3[3, n:])


def reduce_scratch(n, extra):
    return [
        pltpu.VMEM((8, n, D), F32),
        pltpu.VMEM((8, D), F32),
        pltpu.VMEM((7, n, D), F32),
        pltpu.VMEM((7, 8, D), F32),
        pltpu.VMEM((4, n + extra, D), F32),
        pltpu.VMEM((4, n + extra, D), F32),
        pltpu.VMEM((8, n, D), F32),
    ]


REDUCE_COPIES = 7 + 7 + 3 + 3 + 7


def row_order(net, base):
    if base == 0:
        return net.x, net.y, lambda first, then: then % 4 * 4 + first % 4
    return net.y, net.x, lambda first, then: first % 4 * 4 + then % 4


def gather_half(net, mine, panel, base, done):
    a, b, slot = row_order(net, base)
    all_rows, up, down = pl.ds(base, HALF), pl.ds(base, QUART), pl.ds(base + QUART, QUART)

    def pair(src, at, rows, plus, minus):
        view = panel.at[at, rows]
        source = view if src is None else src.at[rows]
        return net.send(source, view, row=plus), net.send(source, view, row=minus)

    def forward(at, rows, row):
        return net.send(panel.at[at, rows], panel.at[at, rows], row=row)

    own = slot(a, b)
    a_plus, a_minus = slot(a + 1, b), slot(a - 1 + 4, b)
    b_plus, b_minus = slot(a, b + 1), slot(a, b - 1 + 4)
    from_left, from_right = pair(mine, own, all_rows, a_plus, a_minus)
    yield
    second = {0: pair(mine, own, all_rows, b_plus, b_minus)}
    yield
    from_left.wait_recv()
    fwd_up = forward(slot(a + 3, b), up, a_plus)
    second[3] = pair(None, slot(a + 3, b), all_rows, b_plus, b_minus)
    from_right.wait_recv()
    fwd_down = forward(slot(a + 1, b), down, a_minus)
    yield
    second[1] = pair(None, slot(a + 1, b), all_rows, b_plus, b_minus)
    done(3, 0)
    done(1, 0)
    third = {}

    def pass_on(o):
        left, right = second[o]
        left.wait_recv()
        f_up = forward(slot(a + o, b + 3), up, b_plus)
        right.wait_recv()
        f_down = forward(slot(a + o, b + 1), down, b_minus)
        third[o] = (f_up, f_down)
        done(o, 3)
        done(o, 1)

    yield
    pass_on(0)
    yield
    fwd_up.wait_recv()
    fwd_down.wait_recv()
    second[2] = pair(None, slot(a + 2, b), all_rows, b_plus, b_minus)
    done(2, 0)
    yield
    pass_on(3)
    yield
    pass_on(1)
    yield
    for copy in third[0]:
        copy.wait_recv()
    done(0, 2)
    yield
    pass_on(2)
    yield
    for o in (3, 1, 2):
        for copy in third[o]:
            copy.wait_recv()
        done(o, 2)
        yield


GATHER_COPIES = 2 + 2 + 4 * 4


def gather_cols(net, mine, panel, done):
    z, k = net.z, net.k
    own = net.c
    plus, minus = (z + 1) % 4 * 2 + k, (z + 3) % 4 * 2 + k
    opposite = (z + 2) % 4 * 2 + k
    sibling = z * 2 + 1 - k
    up, down = pl.ds(0, HALF), pl.ds(HALF, HALF)
    left = net.send(mine, panel.at[own], col=plus)
    right = net.send(mine, panel.at[own], col=minus)
    pair = [net.send(mine, panel.at[own], col=sibling)]
    yield
    left.wait_recv()
    f_up = net.send(panel.at[minus, up], panel.at[minus, up], col=plus)
    pair.append(net.send(panel.at[minus], panel.at[minus], col=sibling))
    right.wait_recv()
    f_down = net.send(panel.at[plus, down], panel.at[plus, down], col=minus)
    pair.append(net.send(panel.at[plus], panel.at[plus], col=sibling))
    done(minus)
    done(plus)
    yield
    f_up.wait_recv()
    f_down.wait_recv()
    pair.append(net.send(panel.at[opposite], panel.at[opposite], col=sibling))
    done(opposite)
    yield
    for o, copy in zip((0, 3, 1, 2), pair):
        copy.wait_recv()
        done((z + o) % 4 * 2 + 1 - k)
    yield


COLS_COPIES = 3 + 4 + 1


def drive(order, **runs):
    def step(name):
        try:
            next(runs[name])
        except StopIteration:
            del runs[name]

    for name in order:
        if name in runs:
            step(name)
    while runs:
        for name in list(runs):
            step(name)


GATHER_ORDER = "abtctabotabtabtctababctababtcabtab"


def gather_kernel(
    x_ref, c_ref, wq_ref, wk_ref, wv_ref,
    xs_ref, cs_ref, att_ref, gq_ref, key_ref, val_ref, gs_ref, gks_ref,
    q_ref, xp, cp, x_stage, c_stage, stage_sem, ssem, rsem, *reduce_refs,
):
    net = Net(ssem, rsem)
    net.barrier()
    ar1, ar2 = reduce_refs[:7], reduce_refs[7:]
    staged = []

    def split_out(source, stage, out, slot):
        @pl.loop(0, BLK)
        def _(i):
            hi, lo = split2(source[pl.ds(pl.multiple_of(i * TILE, TILE), TILE), :])
            stage[slot, i, 0:TILE, :] = hi
            stage[slot, i, TILE : 2 * TILE, :] = lo

        copy = pltpu.make_async_copy(stage.at[slot], out.at[slot], stage_sem.at[len(staged)])
        copy.start()
        staged.append(copy)

    seen = set()

    def x_done(dx, dy):
        if (dx, dy) in seen:
            slot = (net.y + dy) % 4 * 4 + (net.x + dx) % 4
            split_out(xp.at[slot], x_stage, xs_ref, slot)
        seen.add((dx, dy))

    def cols_done(slot):
        split_out(cp.at[slot], c_stage, cs_ref, slot)

    def attention():
        def first(i, sums):
            state, key_sum = sums
            rows = pl.ds(pl.multiple_of(i * CH, CH), CH)
            x = x_ref[rows, :]
            q_ref[rows, :] = dot(x, wq_ref[...])
            key = dot(x, wk_ref[...])
            val = dot(x, wv_ref[...])
            key_ref[rows, :] = key
            val_ref[rows, :] = val
            feat_k = feat(key)
            return state + dot(feat_k, val, TN), key_sum + jnp.sum(feat_k, axis=0, keepdims=True)

        zero = (jnp.zeros((D, D), F32), jnp.zeros((1, D), F32))
        state, key_sum = lax.fori_loop(0, NODE // CH, first, zero)
        ar1[0][...] = state.reshape(8, 32, D)
        ar1[1][...] = jnp.broadcast_to(key_sum, (8, D))
        yield from all_reduce(net, *ar1)
        state = ar1[6][...].reshape(D, D)
        key_row = key_total(ar1[5], 32)[0:1]

        def second(i, sums):
            grad_state, grad_key_sum = sums
            rows = pl.ds(pl.multiple_of(i * CH, CH), CH)
            q = q_ref[rows, :]
            cot = c_ref[rows, :]
            feat_q = feat(q)
            den = jnp.sum(feat_q * key_row, axis=1, keepdims=True)
            att = dot(feat_q, state) / den
            att_ref[rows, :] = att
            scaled = cot / den
            weight_dot = jnp.sum(cot * att, axis=1, keepdims=True) / den
            gq_ref[rows, :] = (dot(scaled, state, NT) - weight_dot * key_row) * slope(q)
            return (
                grad_state + dot(feat_q, scaled, TN),
                grad_key_sum - jnp.sum(feat_q * weight_dot, axis=0, keepdims=True),
            )

        grad_state, grad_key_sum = lax.fori_loop(0, NODE // CH, second, zero)
        ar2[0][...] = grad_state.reshape(8, 32, D)
        ar2[1][...] = jnp.broadcast_to(grad_key_sum, (8, D))
        yield from all_reduce(net, *ar2)
        gs_ref[...] = ar2[6][...].reshape(D, D)
        gks_ref[...] = key_total(ar2[5], 32)

    def own_blocks():
        yield
        split_out(x_ref, x_stage, xs_ref, net.r)
        split_out(c_ref, c_stage, cs_ref, net.c)

    drive(
        GATHER_ORDER,
        a=gather_half(net, x_ref, xp, 0, x_done),
        b=gather_half(net, x_ref, xp, HALF, lambda dy, dx: x_done(dx, dy)),
        c=gather_cols(net, c_ref, cp, cols_done),
        t=attention(),
        o=own_blocks(),
    )
    net.finish()
    for copy in staged:
        copy.wait()


def run_gather(x, cot, wq, wk, wv):
    copies = 2 * GATHER_COPIES + COLS_COPIES + 2 * REDUCE_COPIES
    block = jax.ShapeDtypeStruct((NODE, D), F32)
    vmem, hbm = pl.BlockSpec(memory_space=pltpu.VMEM), pl.BlockSpec(memory_space=pl.ANY)
    return pl.pallas_call(
        gather_kernel,
        out_shape=[
            jax.ShapeDtypeStruct((16, BLK, 2 * TILE, D), BF16),
            jax.ShapeDtypeStruct((8, BLK, 2 * TILE, D), BF16),
            block, block, block, block,
            jax.ShapeDtypeStruct((D, D), F32),
            jax.ShapeDtypeStruct((8, D), F32),
        ],
        in_specs=[vmem] * 5,
        out_specs=[hbm, hbm] + [vmem] * 6,
        scratch_shapes=[
            pltpu.VMEM((NODE, D), F32),
            pltpu.VMEM((16, NODE, D), F32),
            pltpu.VMEM((8, NODE, D), F32),
            pltpu.VMEM((16, BLK, 2 * TILE, D), BF16),
            pltpu.VMEM((8, BLK, 2 * TILE, D), BF16),
            pltpu.SemaphoreType.DMA((24,)),
            pltpu.SemaphoreType.DMA((copies,)),
            pltpu.SemaphoreType.DMA((copies,)),
        ]
        + reduce_scratch(32, 8)
        + reduce_scratch(32, 8),
        compiler_params=pltpu.CompilerParams(
            collective_id=0, has_side_effects=True, vmem_limit_bytes=60 * 2**20
        ),
        name="gather",
    )(x, cot, wq, wk, wv)


CHUNK = 16
SLOTS = 3
GROUP = 16


def tile_kernel(
    rows_ref, cols_ref, count_ref, tiles_ref, xs_ref, cs_ref,
    f_ref, t_ref,
    xs, cs, f, t, buf, sem, tile_sem,
):
    count = count_ref[0]
    chunks = (count + CHUNK - 1) // CHUNK
    load_c = pltpu.make_async_copy(cs_ref, cs, sem.at[0])
    load_x = pltpu.make_async_copy(xs_ref, xs, sem.at[1])

    def fetch(chunk, slot):
        return pltpu.make_async_copy(
            tiles_ref.at[pl.ds(chunk * CHUNK, CHUNK)], buf.at[slot], tile_sem.at[slot]
        )

    def sweep(body):
        for i in range(SLOTS - 1):
            @pl.when(i < chunks)
            def _(i=i):
                fetch(i, i).start()

        @pl.loop(0, chunks)
        def _(chunk):
            slot = chunk % SLOTS

            @pl.when(chunk + SLOTS - 1 < chunks)
            def _():
                fetch(chunk + SLOTS - 1, (chunk + SLOTS - 1) % SLOTS).start()

            fetch(chunk, slot).wait()

            @pl.loop(0, CHUNK // GROUP)
            def _(group):
                first = group * GROUP
                for i in range(GROUP):
                    at = chunk * CHUNK + first + i
                    tile = buf[slot, first + i]
                    body(jnp.where(at < count, tile, 0.0), rows_ref[at], cols_ref[at])

    def product(tile, panel):
        hi, lo = split2(tile)
        whole = jnp.dot(jnp.concatenate([hi, hi], axis=1), panel, preferred_element_type=F32)
        return whole + jnp.dot(lo, panel[0:TILE], preferred_element_type=F32)

    def backward(tile, row, col):
        t[col] += product(tile.T, cs[row])

    def forward(tile, row, col):
        f[row] += product(tile, xs[col])

    load_c.start()
    load_x.start()
    t[...] = jnp.zeros_like(t)
    f[...] = jnp.zeros_like(f)
    load_c.wait()
    sweep(backward)
    store_t = pltpu.make_async_copy(t, t_ref, sem.at[2])
    store_t.start()
    load_x.wait()
    sweep(forward)
    store_f = pltpu.make_async_copy(f, f_ref, sem.at[3])
    store_f.start()
    store_t.wait()
    store_f.wait()


def run_tiles(tile_rows, tile_cols, tile_count, tiles, xs, cs):
    hbm, smem = pl.BlockSpec(memory_space=pl.ANY), pl.BlockSpec(memory_space=pltpu.SMEM)
    return pl.pallas_call(
        tile_kernel,
        out_shape=[
            jax.ShapeDtypeStruct((8 * BLK, TILE, D), F32),
            jax.ShapeDtypeStruct((16 * BLK, TILE, D), F32),
        ],
        in_specs=[smem] * 3 + [hbm] * 3,
        out_specs=[hbm] * 2,
        scratch_shapes=[
            pltpu.VMEM((16 * BLK, 2 * TILE, D), BF16),
            pltpu.VMEM((8 * BLK, 2 * TILE, D), BF16),
            pltpu.VMEM((8 * BLK, TILE, D), F32),
            pltpu.VMEM((16 * BLK, TILE, D), F32),
            pltpu.VMEM((SLOTS, CHUNK, TILE, TILE), F32),
            pltpu.SemaphoreType.DMA((4,)),
            pltpu.SemaphoreType.DMA((SLOTS,)),
        ],
        compiler_params=pltpu.CompilerParams(vmem_limit_bytes=60 * 2**20),
        name="tiles",
    )(
        tile_rows, tile_cols, tile_count, tiles,
        xs.reshape(16 * BLK, 2 * TILE, D), cs.reshape(8 * BLK, 2 * TILE, D),
    )


def scatter_half(net, t_hbm, t, base, leaf, main, leaf2, main2, own_ref, ready):
    s, b, slot = row_order(net, base)
    up, down, both = pl.ds(base, QUART), pl.ds(base + QUART, QUART), pl.ds(base, HALF)
    order = (2, 1, 3, 0)
    b_plus, b_minus = slot(s, b + 1), slot(s, b + 3)
    leaves, mains = [], []
    for i, o in enumerate(order):
        at = slot(s + o, b + 2)
        leaves.append(
            (
                net.send(t_hbm.at[at, up], leaf.at[i, 0], row=b_plus),
                net.send(t_hbm.at[at, down], leaf.at[i, 1], row=b_minus),
            )
        )
        if i == 1:
            yield
    s_plus, s_minus = slot(s + 1, b), slot(s + 3, b)

    def main_sends(i):
        for copy in leaves[i]:
            copy.wait_recv()
        plus, minus = slot(s + order[i], b + 1), slot(s + order[i], b + 3)
        t[plus, up] += leaf[i, 0]
        t[minus, down] += leaf[i, 1]
        return (
            net.send(t.at[plus, both], main.at[i, 0], row=b_plus),
            net.send(t.at[minus, both], main.at[i, 1], row=b_minus),
        )

    def collect(i):
        for copy in mains[i]:
            copy.wait_recv()
        at = slot(s + order[i], b)
        t[at, both] += main[i, 0] + main[i, 1]
        return at

    yield
    ready()
    mains.append(main_sends(0))
    yield
    mains.append(main_sends(1))
    yield
    mains.append(main_sends(2))
    yield
    at = collect(0)
    leaves2 = (
        net.send(t.at[at, up], leaf2.at[0], row=s_plus),
        net.send(t.at[at, down], leaf2.at[1], row=s_minus),
    )
    yield
    mains.append(main_sends(3))
    yield
    collect(1)
    yield
    collect(2)
    for copy in leaves2:
        copy.wait_recv()
    t[s_plus, up] += leaf2[0]
    t[s_minus, down] += leaf2[1]
    mains2 = (
        net.send(t.at[s_plus, both], main2.at[0], row=s_plus),
        net.send(t.at[s_minus, both], main2.at[1], row=s_minus),
    )
    yield
    collect(3)
    yield
    for copy in mains2:
        copy.wait_recv()
    own_ref[both, :] = t[slot(s, b), both] + (main2[0] + main2[1])


SCATTER_COPIES = GATHER_COPIES


def scatter_cols(net, f_hbm, f, pair, leaf, main, ready):
    z, k = net.z, net.k
    up, down = pl.ds(0, HALF), pl.ds(HALF, HALF)
    order = (2, 1, 3, 0)
    copies = [
        net.send(f_hbm.at[(z + o) % 4 * 2 + 1 - k], pair.at[i], col=z * 2 + 1 - k)
        for i, o in enumerate(order)
    ]
    yield
    ready()
    plus, minus = (z + 1) % 4 * 2 + k, (z + 3) % 4 * 2 + k
    for i, o in enumerate(order):
        copies[i].wait_recv()
        at = (z + o) % 4 * 2 + k
        f[at] += pair[i]
        if o == 2:
            leaves = (
                net.send(f.at[at, up], leaf.at[0], col=plus),
                net.send(f.at[at, down], leaf.at[1], col=minus),
            )
            yield
    yield
    for copy in leaves:
        copy.wait_recv()
    f[plus, up] += leaf[0]
    f[minus, down] += leaf[1]
    mains = (
        net.send(f.at[plus], main.at[0], col=plus),
        net.send(f.at[minus], main.at[1], col=minus),
    )
    yield
    for copy in mains:
        copy.wait_recv()
    f[net.c] += main[0] + main[1]


SCATTER_COLS_COPIES = 4 + 2 + 2


SCATTER_ORDER = "abgtabttgabgtabgtababtabgabtgabgabgabg"


def scatter_kernel(
    x_ref, c_ref, wq_ref, wk_ref, wv_ref, wg_ref,
    att_ref, gq_ref, key_ref, val_ref, gs_ref, gks_ref, f_hbm, t_hbm,
    own_ref, out_ref, gx_ref, dq_ref, dk_ref, dv_ref, dg_ref,
    f, t, leaf, main, leaf2, main2, pair, zleaf, zmain, load_sem, ssem, rsem, *reduce_refs,
):
    net = Net(ssem, rsem)
    load_t = pltpu.make_async_copy(t_hbm, t, load_sem.at[0])
    load_f = pltpu.make_async_copy(f_hbm, f, load_sem.at[1])
    load_t.start()
    load_f.start()
    net.barrier()
    ar1, ar2 = reduce_refs[:7], reduce_refs[7:]

    def ready(copy):
        pending = [copy]

        def once():
            if pending:
                pending.pop().wait()

        return once

    def attention():
        for i in range(NODE // CH):
            rows = pl.ds(i * CH, CH)
            x = x_ref[rows, :]
            key = key_ref[rows, :]
            gq = gq_ref[rows, :]
            gk = (dot(val_ref[rows, :], gs_ref[...], NT) + gks_ref[0:1, :]) * slope(key)
            gv = dot(feat(key), gs_ref[...])
            gx = dot(gq, wq_ref[...], NT) + dot(gk, wk_ref[...], NT)
            gx_ref[rows, :] = gx + dot(gv, wv_ref[...], NT)
            for j, grad in enumerate((gq, gk, gv)):
                product = dot(x, grad, TN).reshape(8, 32, D)
                at = pl.ds(32 * j, 32)
                ar1[0][:, at, :] = product if i == 0 else ar1[0][:, at, :] + product
            yield
        yield from all_reduce(net, ar1[0], None, *ar1[2:])
        for j, grad in enumerate((dq_ref, dk_ref, dv_ref)):
            grad[...] = ar1[6][:, pl.ds(32 * j, 32), :].reshape(D, D)

    def graph():
        yield from scatter_cols(net, f_hbm, f, pair, zleaf, zmain, ready(load_f))
        dg_ref[...] = jnp.zeros((D, D), F32)

        @pl.loop(0, NODE // CH)
        def _(i):
            rows = pl.ds(pl.multiple_of(i * CH, CH), CH)
            mixed = f[net.c, rows, :]
            out_ref[rows, :] = att_ref[rows, :] + dot(mixed, wg_ref[...])
            dg_ref[...] += dot(mixed, c_ref[rows, :], TN)

        ar2[0][...] = dg_ref[...].reshape(8, 32, D)
        yield from all_reduce(net, ar2[0], None, *ar2[2:])
        dg_ref[...] = ar2[6][...].reshape(D, D)

    once_t = ready(load_t)

    def half(i):
        return scatter_half(
            net, t_hbm, t, i * HALF, leaf.at[i], main.at[i], leaf2.at[i], main2.at[i], own_ref, once_t
        )

    drive(SCATTER_ORDER, a=half(0), b=half(1), g=graph(), t=attention())
    net.finish()


def run_scatter(x, cot, wq, wk, wv, wg, att, gq, key, val, gs, gks, f, t):
    copies = 2 * SCATTER_COPIES + SCATTER_COLS_COPIES + 2 * REDUCE_COPIES
    block, weight = jax.ShapeDtypeStruct((NODE, D), F32), jax.ShapeDtypeStruct((D, D), F32)
    vmem, hbm = pl.BlockSpec(memory_space=pltpu.VMEM), pl.BlockSpec(memory_space=pl.ANY)
    return pl.pallas_call(
        scatter_kernel,
        out_shape=[block, block, block, weight, weight, weight, weight],
        in_specs=[vmem] * 12 + [hbm] * 2,
        out_specs=[vmem] * 7,
        scratch_shapes=[
            pltpu.VMEM((8, NODE, D), F32),
            pltpu.VMEM((16, NODE, D), F32),
            pltpu.VMEM((2, 4, 2, QUART, D), F32),
            pltpu.VMEM((2, 4, 2, HALF, D), F32),
            pltpu.VMEM((2, 2, QUART, D), F32),
            pltpu.VMEM((2, 2, HALF, D), F32),
            pltpu.VMEM((4, NODE, D), F32),
            pltpu.VMEM((2, HALF, D), F32),
            pltpu.VMEM((2, NODE, D), F32),
            pltpu.SemaphoreType.DMA((2,)),
            pltpu.SemaphoreType.DMA((copies,)),
            pltpu.SemaphoreType.DMA((copies,)),
        ]
        + reduce_scratch(96, 0)
        + reduce_scratch(32, 0),
        compiler_params=pltpu.CompilerParams(
            collective_id=1, has_side_effects=True, vmem_limit_bytes=60 * 2**20
        ),
        name="scatter",
    )(x, cot, wq, wk, wv, wg, att, gq, key, val, gs, gks, f, t)


def finish_kernel(own_hbm, wg_ref, *refs):
    taken, given, held, (own, load_sem, store_sem) = refs[:6], refs[6:12], refs[12:18], refs[18:]
    loads = [pltpu.make_async_copy(own_hbm, own, load_sem.at[6])]
    for i in range(6):
        loads.append(pltpu.make_async_copy(taken[i], held[i], load_sem.at[i]))
    for copy in loads:
        copy.start()
    stores = [pltpu.make_async_copy(held[i], given[i], store_sem.at[i]) for i in range(6)]
    loads[0].wait()
    term = dot(own[...], wg_ref[...], NT)
    loads[1].wait()
    held[0][...] += term
    stores[0].start()
    for i in range(1, 6):
        loads[i + 1].wait()
        stores[i].start()
    for copy in stores:
        copy.wait()


def run_finish(own, wg, out, gx, *weights):
    vmem, hbm = pl.BlockSpec(memory_space=pltpu.VMEM), pl.BlockSpec(memory_space=pl.ANY)
    gx, out, *weights = pl.pallas_call(
        finish_kernel,
        out_shape=[jax.ShapeDtypeStruct(a.shape, F32) for a in (gx, out, *weights)],
        in_specs=[hbm, vmem] + [hbm] * 6,
        out_specs=[hbm] * 6,
        scratch_shapes=[
            *[pltpu.VMEM(a.shape, F32) for a in (gx, out, *weights)],
            pltpu.VMEM((NODE, D), F32),
            pltpu.SemaphoreType.DMA((7,)),
            pltpu.SemaphoreType.DMA((6,)),
        ],
        compiler_params=pltpu.CompilerParams(vmem_limit_bytes=60 * 2**20),
        name="finish",
    )(own, wg, gx, out, *weights)
    return (out, gx, *weights)


def per_device(x, cot, wq, wk, wv, wg, tiles, tile_rows, tile_cols, tile_count):
    xs, cs, att, gq, key, val, gs, gks = run_gather(x, cot, wq, wk, wv)
    f, t = run_tiles(tile_rows, tile_cols, tile_count, tiles, xs, cs)
    f, t = f.reshape(8, NODE, D), t.reshape(16, NODE, D)
    own, *results = run_scatter(x, cot, wq, wk, wv, wg, att, gq, key, val, gs, gks, f, t)
    return run_finish(own, wg, *results)


def solution(mesh):
    nodes = P(("rows", "cols"), None)
    slots = P(("rows", "cols"))
    return jax.shard_map(
        per_device,
        mesh=mesh,
        in_specs=(nodes, nodes, P(), P(), P(), P(), P(("rows", "cols"), None, None), slots, slots, slots),
        out_specs=(nodes, nodes, P(), P(), P(), P()),
        check_vma=False,
    )
```

```python
import jax
import jax.numpy as jnp
from jax import lax
from jax.experimental import pallas as pl
from jax.experimental.pallas import tpu as pltpu
from jax.sharding import PartitionSpec as P

MESH = pl.DeviceIdType.MESH
F32, BF16 = jnp.float32, jnp.bfloat16
TILE, D, NODE, MAXT = 128, 256, 768, 288
HALF, QUART = NODE // 2, NODE // 4
BLK = NODE // TILE
CH = 384
NN, NT, TN = ((1,), (0,)), ((1,), (1,)), ((0,), (0,))


def dot(a, b, dims=NN):
    (a_hi, a_lo), (b_hi, b_lo) = split2(a), split2(b)

    def one(p, q):
        return lax.dot_general(p, q, (dims, ((), ())), preferred_element_type=F32)

    return one(a_hi, b_hi) + (one(a_hi, b_lo) + one(a_lo, b_hi))


def feat(v):
    return jnp.where(v > 0, v + 1.0, jnp.exp(jnp.minimum(v, 0.0)))


def slope(v):
    return jnp.where(v > 0, 1.0, jnp.exp(jnp.minimum(v, 0.0)))


def split2(v):
    hi = v.astype(BF16)
    return hi, (v - hi.astype(F32)).astype(BF16)


class Net:
    def __init__(self, ssem, rsem):
        self.ssem, self.rsem, self.n, self.sent = ssem, rsem, 0, []
        self.r, self.c = lax.axis_index("rows"), lax.axis_index("cols")
        self.y, self.x = self.r // 4, self.r % 4
        self.z, self.k = self.c // 2, self.c % 2

    def send(self, src, dst, row=None, col=None):
        i, self.n = self.n, self.n + 1
        copy = pltpu.make_async_remote_copy(
            src_ref=src,
            dst_ref=dst,
            send_sem=self.ssem.at[i],
            recv_sem=self.rsem.at[i],
            device_id=(self.r if row is None else row, self.c if col is None else col),
            device_id_type=MESH,
        )
        copy.start()
        self.sent.append(copy)
        return copy

    def barrier(self):
        sem = pltpu.get_barrier_semaphore()
        there = [(self.r, (self.c + j) % 8) for j in range(1, 8)]
        there += [(self.y * 4 + (self.x + j) % 4, self.c) for j in range(1, 4)]
        there += [((self.y + j) % 4 * 4 + self.x, self.c) for j in range(1, 4)]
        for device in there:
            pl.semaphore_signal(sem, inc=1, device_id=device, device_id_type=MESH)
        pl.semaphore_wait(sem, len(there))

    def finish(self):
        for copy in self.sent:
            copy.wait_send()


def all_reduce(net, part, key, r1, kbuf, r2, r3, full):
    c, x, y = net.c, net.x, net.y
    n = part.shape[1]
    first = [net.send(part.at[(c + j) % 8], r1.at[j - 1], col=(c + j) % 8) for j in range(1, 8)]
    if key is not None:
        first += [net.send(key, kbuf.at[j - 1], col=(c + j) % 8) for j in range(1, 8)]
    yield
    for copy in first:
        copy.wait_recv()
    total = part[c]
    for j in range(7):
        total = total + r1[j]
    r2[x, 0:n] = total
    if key is not None:
        total = key[...]
        for j in range(7):
            total = total + kbuf[j]
        r2[x, n:] = total
    second = [net.send(r2.at[x], r2.at[x], row=y * 4 + (x + j) % 4) for j in range(1, 4)]
    yield
    for copy in second:
        copy.wait_recv()
    r3[y] = (r2[0] + r2[1]) + (r2[2] + r2[3])
    third = [net.send(r3.at[y], r3.at[y], row=(y + j) % 4 * 4 + x) for j in range(1, 4)]
    yield
    for copy in third:
        copy.wait_recv()
    full[c] = (r3[0, 0:n] + r3[1, 0:n]) + (r3[2, 0:n] + r3[3, 0:n])
    fourth = [net.send(full.at[c], full.at[c], col=(c + j) % 8) for j in range(1, 8)]
    yield
    for copy in fourth:
        copy.wait_recv()


def key_total(r3, n):
    return (r3[0, n:] + r3[1, n:]) + (r3[2, n:] + r3[3, n:])


def reduce_scratch(n, extra):
    return [
        pltpu.VMEM((8, n, D), F32),
        pltpu.VMEM((8, D), F32),
        pltpu.VMEM((7, n, D), F32),
        pltpu.VMEM((7, 8, D), F32),
        pltpu.VMEM((4, n + extra, D), F32),
        pltpu.VMEM((4, n + extra, D), F32),
        pltpu.VMEM((8, n, D), F32),
    ]


REDUCE_COPIES = 7 + 7 + 3 + 3 + 7


def row_order(net, base):
    if base == 0:
        return net.x, net.y, lambda first, then: then % 4 * 4 + first % 4
    return net.y, net.x, lambda first, then: first % 4 * 4 + then % 4


def gather_half(net, mine, panel, base, done, keep):
    a, b, slot = row_order(net, base)
    all_rows, up, down = pl.ds(base, HALF), pl.ds(base, QUART), pl.ds(base + QUART, QUART)

    def pair(src, at, rows, plus, minus):
        view = panel.at[at, rows]
        source = view if src is None else src.at[rows]
        return net.send(source, view, row=plus), net.send(source, view, row=minus)

    def forward(at, rows, row):
        return net.send(panel.at[at, rows], panel.at[at, rows], row=row)

    own = slot(a, b)
    a_plus, a_minus = slot(a + 1, b), slot(a - 1 + 4, b)
    b_plus, b_minus = slot(a, b + 1), slot(a, b - 1 + 4)
    from_left, from_right = pair(mine, own, all_rows, a_plus, a_minus)
    yield
    second = {0: pair(mine, own, all_rows, b_plus, b_minus)}
    yield
    from_left.wait_recv()
    fwd_up = forward(slot(a + 3, b), up, a_plus)
    second[3] = pair(None, slot(a + 3, b), all_rows, b_plus, b_minus)
    from_right.wait_recv()
    fwd_down = forward(slot(a + 1, b), down, a_minus)
    yield
    second[1] = pair(None, slot(a + 1, b), all_rows, b_plus, b_minus)
    done(3, 0)
    done(1, 0)

    def pass_on(o):
        left, right = second[o]
        left.wait_recv()
        keep(0, o, panel.at[slot(a + o, b + 3), up])
        right.wait_recv()
        keep(1, o, panel.at[slot(a + o, b + 1), down])
        done(o, 3)
        done(o, 1)

    yield
    pass_on(0)
    yield
    fwd_up.wait_recv()
    fwd_down.wait_recv()
    second[2] = pair(None, slot(a + 2, b), all_rows, b_plus, b_minus)
    done(2, 0)
    yield
    pass_on(3)
    yield
    pass_on(1)
    yield
    pass_on(2)


GATHER_COPIES = 2 + 2 + 4 * 2


def gather_cols(net, mine, panel, done):
    z, k = net.z, net.k
    own = net.c
    plus, minus = (z + 1) % 4 * 2 + k, (z + 3) % 4 * 2 + k
    opposite = (z + 2) % 4 * 2 + k
    sibling = z * 2 + 1 - k
    up, down = pl.ds(0, HALF), pl.ds(HALF, HALF)
    left = net.send(mine, panel.at[own], col=plus)
    right = net.send(mine, panel.at[own], col=minus)
    pair = [net.send(mine, panel.at[own], col=sibling)]
    yield
    left.wait_recv()
    f_up = net.send(panel.at[minus, up], panel.at[minus, up], col=plus)
    pair.append(net.send(panel.at[minus], panel.at[minus], col=sibling))
    right.wait_recv()
    f_down = net.send(panel.at[plus, down], panel.at[plus, down], col=minus)
    pair.append(net.send(panel.at[plus], panel.at[plus], col=sibling))
    done(minus)
    done(plus)
    yield
    f_up.wait_recv()
    f_down.wait_recv()
    pair.append(net.send(panel.at[opposite], panel.at[opposite], col=sibling))
    done(opposite)
    yield
    for o, copy in zip((0, 3, 1, 2), pair):
        copy.wait_recv()
        done((z + o) % 4 * 2 + 1 - k)
    yield


COLS_COPIES = 3 + 4 + 1


def drive(order, **runs):
    def step(name):
        try:
            next(runs[name])
        except StopIteration:
            del runs[name]

    for name in order:
        if name in runs:
            step(name)
    while runs:
        for name in list(runs):
            step(name)


GATHER_ORDER = "abtctabotabtabtctbtaababctabctabtab"


def gather_kernel(
    x_ref, c_ref, wq_ref, wk_ref, wv_ref,
    xs_ref, cs_ref, last0, last1, last2, last3, att_ref, gq_ref, key_ref, val_ref, gs_ref, gks_ref,
    q_ref, xp, cp, x_stage, c_stage, stage_sem, ssem, rsem, *reduce_refs,
):
    net = Net(ssem, rsem)
    net.barrier()
    last_refs = (last0, last1, last2, last3)
    ar1, ar2 = reduce_refs[:7], reduce_refs[7:]
    staged = []

    def send_out(source, target):
        copy = pltpu.make_async_copy(source, target, stage_sem.at[len(staged)])
        copy.start()
        staged.append(copy)

    def split_out(source, stage, out, slot, first=0, blocks=BLK):
        @pl.loop(first, first + blocks)
        def _(i):
            hi, lo = split2(source[pl.ds(pl.multiple_of(i * TILE, TILE), TILE), :])
            stage[slot, i, 0:TILE, :] = hi
            stage[slot, i, TILE : 2 * TILE, :] = lo

        at = pl.ds(first, blocks)
        send_out(stage.at[slot, at], out.at[slot, at])

    def x_done(half, dx, dy):
        slot = (net.y + dy) % 4 * 4 + (net.x + dx) % 4
        split_out(xp.at[slot], x_stage, xs_ref, slot, half * BLK // 2, BLK // 2)

    def keep(half):
        return lambda way, o, source: send_out(source, last_refs[2 * half + way].at[o])

    def cols_done(slot):
        split_out(cp.at[slot], c_stage, cs_ref, slot)

    def attention():
        def first(i, sums):
            state, key_sum = sums
            rows = pl.ds(pl.multiple_of(i * CH, CH), CH)
            x = x_ref[rows, :]
            q_ref[rows, :] = dot(x, wq_ref[...])
            key = dot(x, wk_ref[...])
            val = dot(x, wv_ref[...])
            key_ref[rows, :] = key
            val_ref[rows, :] = val
            feat_k = feat(key)
            return state + dot(feat_k, val, TN), key_sum + jnp.sum(feat_k, axis=0, keepdims=True)

        zero = (jnp.zeros((D, D), F32), jnp.zeros((1, D), F32))
        state, key_sum = lax.fori_loop(0, NODE // CH, first, zero)
        ar1[0][...] = state.reshape(8, 32, D)
        ar1[1][...] = jnp.broadcast_to(key_sum, (8, D))
        yield from all_reduce(net, *ar1)
        state = ar1[6][...].reshape(D, D)
        key_row = key_total(ar1[5], 32)[0:1]

        def second(i, sums):
            grad_state, grad_key_sum = sums
            rows = pl.ds(pl.multiple_of(i * CH, CH), CH)
            q = q_ref[rows, :]
            cot = c_ref[rows, :]
            feat_q = feat(q)
            den = jnp.sum(feat_q * key_row, axis=1, keepdims=True)
            att = dot(feat_q, state) / den
            att_ref[rows, :] = att
            scaled = cot / den
            weight_dot = jnp.sum(cot * att, axis=1, keepdims=True) / den
            gq_ref[rows, :] = (dot(scaled, state, NT) - weight_dot * key_row) * slope(q)
            return (
                grad_state + dot(feat_q, scaled, TN),
                grad_key_sum - jnp.sum(feat_q * weight_dot, axis=0, keepdims=True),
            )

        grad_state, grad_key_sum = lax.fori_loop(0, NODE // CH, second, zero)
        ar2[0][...] = grad_state.reshape(8, 32, D)
        ar2[1][...] = jnp.broadcast_to(grad_key_sum, (8, D))
        yield from all_reduce(net, *ar2)
        gs_ref[...] = ar2[6][...].reshape(D, D)
        gks_ref[...] = key_total(ar2[5], 32)

    def own_blocks():
        yield
        split_out(x_ref, x_stage, xs_ref, net.r)
        split_out(c_ref, c_stage, cs_ref, net.c)

    drive(
        GATHER_ORDER,
        a=gather_half(net, x_ref, xp, 0, lambda dx, dy: x_done(0, dx, dy), keep(0)),
        b=gather_half(net, x_ref, xp, HALF, lambda dy, dx: x_done(1, dx, dy), keep(1)),
        c=gather_cols(net, c_ref, cp, cols_done),
        t=attention(),
        o=own_blocks(),
    )
    net.finish()
    for copy in staged:
        copy.wait()


def run_gather(x, cot, wq, wk, wv):
    copies = 2 * GATHER_COPIES + COLS_COPIES + 2 * REDUCE_COPIES
    block = jax.ShapeDtypeStruct((NODE, D), F32)
    vmem, hbm = pl.BlockSpec(memory_space=pltpu.VMEM), pl.BlockSpec(memory_space=pl.ANY)
    return pl.pallas_call(
        gather_kernel,
        out_shape=[
            jax.ShapeDtypeStruct((16, BLK, 2 * TILE, D), BF16),
            jax.ShapeDtypeStruct((8, BLK, 2 * TILE, D), BF16),
            *[jax.ShapeDtypeStruct((4, QUART, D), F32)] * 4,
            block, block, block, block,
            jax.ShapeDtypeStruct((D, D), F32),
            jax.ShapeDtypeStruct((8, D), F32),
        ],
        in_specs=[vmem] * 5,
        out_specs=[hbm] * 6 + [vmem] * 6,
        scratch_shapes=[
            pltpu.VMEM((NODE, D), F32),
            pltpu.VMEM((16, NODE, D), F32),
            pltpu.VMEM((8, NODE, D), F32),
            pltpu.VMEM((16, BLK, 2 * TILE, D), BF16),
            pltpu.VMEM((8, BLK, 2 * TILE, D), BF16),
            pltpu.SemaphoreType.DMA((2 * 11 + 16 + 9,)),
            pltpu.SemaphoreType.DMA((copies,)),
            pltpu.SemaphoreType.DMA((copies,)),
        ]
        + reduce_scratch(32, 8)
        + reduce_scratch(32, 8),
        compiler_params=pltpu.CompilerParams(
            collective_id=0, has_side_effects=True, vmem_limit_bytes=60 * 2**20
        ),
        name="gather",
    )(x, cot, wq, wk, wv)


CHUNK = 16
SLOTS = 3


def sweep(count, rows_ref, cols_ref, tiles_ref, buf, tile_sem, body):
    chunks = (count + CHUNK - 1) // CHUNK

    def fetch(chunk, slot):
        return pltpu.make_async_copy(
            tiles_ref.at[pl.ds(chunk * CHUNK, CHUNK)], buf.at[slot], tile_sem.at[slot]
        )

    for i in range(SLOTS - 1):
        @pl.when(i < chunks)
        def _(i=i):
            fetch(i, i).start()

    @pl.loop(0, chunks)
    def _(chunk):
        slot = chunk % SLOTS

        @pl.when(chunk + SLOTS - 1 < chunks)
        def _():
            fetch(chunk + SLOTS - 1, (chunk + SLOTS - 1) % SLOTS).start()

        fetch(chunk, slot).wait()
        for i in range(CHUNK):
            at = chunk * CHUNK + i
            tile = buf[slot, i]
            body(jnp.where(at < count, tile, 0.0), rows_ref[at], cols_ref[at])


def product(tile, panel):
    hi, lo = split2(tile)
    whole = jnp.dot(jnp.concatenate([hi, hi], axis=1), panel, preferred_element_type=F32)
    return whole + jnp.dot(lo, panel[0:TILE], preferred_element_type=F32)


def block_rows(block):
    return pl.ds(pl.multiple_of(block * TILE, TILE), TILE)


def backward_kernel(
    rows_ref, cols_ref, count_ref, place_ref, tiles_ref, cs_ref,
    t_ref, leaf0, leaf1, leaf2, leaf3,
    cs, t, buf, sem, tile_sem,
):
    load = pltpu.make_async_copy(cs_ref, cs, sem.at[0])
    load.start()
    t[...] = jnp.zeros_like(t)
    load.wait()

    def body(tile, row, col):
        t[block_rows(col), :] += product(tile.T, cs[row])

    sweep(count_ref[0], rows_ref, cols_ref, tiles_ref, buf, tile_sem, body)
    y, x = place_ref[0], place_ref[1]
    stores = [pltpu.make_async_copy(t, t_ref, sem.at[0])]
    for kind, leaf in enumerate((leaf0, leaf1, leaf2, leaf3)):
        for i, o in enumerate(SCATTER_TURNS):
            dx, dy = (o, 2) if kind < 2 else (2, o)
            slot = (y + dy) % 4 * 4 + (x + dx) % 4
            source = t.at[pl.ds(pl.multiple_of(slot * NODE + kind * QUART, QUART), QUART)]
            stores.append(pltpu.make_async_copy(source, leaf.at[i], sem.at[1 + 4 * kind + i]))
    for copy in stores:
        copy.start()
    for copy in stores:
        copy.wait()


def forward_kernel(
    rows_ref, cols_ref, count_ref, place_ref, tiles_ref, xs_ref, last0, last1, last2, last3,
    f_ref,
    xs, f, late, buf, sem, tile_sem,
):
    load = pltpu.make_async_copy(xs_ref, xs, sem.at[0])
    loads = [
        pltpu.make_async_copy(last, late.at[kind], sem.at[1 + kind])
        for kind, last in enumerate((last0, last1, last2, last3))
    ]
    for copy in loads + [load]:
        copy.start()
    f[...] = jnp.zeros_like(f)
    for copy in loads + [load]:
        copy.wait()
    y, x = place_ref[0], place_ref[1]
    for kind in range(4):
        for o in range(4):
            dx, dy = (o, 2) if kind < 2 else (2, o)
            slot = (y + dy) % 4 * 4 + (x + dx) % 4
            for part in range(0, QUART, PART):
                block, at = divmod(kind * QUART + part, TILE)
                hi, lo = split2(late[kind, o, part : part + PART, :])
                xs[slot * BLK + block, at : at + PART, :] = hi
                xs[slot * BLK + block, TILE + at : TILE + at + PART, :] = lo

    def body(tile, row, col):
        f[block_rows(row), :] += product(tile, xs[col])

    sweep(count_ref[0], rows_ref, cols_ref, tiles_ref, buf, tile_sem, body)
    store = pltpu.make_async_copy(f, f_ref, sem.at[0])
    store.start()
    store.wait()


PART = 64
SCATTER_TURNS = (2, 1, 3, 0)


def run_sweep(kernel, name, out_shape, scratch, sems, scalars, tiles, *panels):
    hbm, smem = pl.BlockSpec(memory_space=pltpu.HBM), pl.BlockSpec(memory_space=pltpu.SMEM)
    return pl.pallas_call(
        kernel,
        out_shape=out_shape,
        in_specs=[smem] * 4 + [hbm] * (1 + len(panels)),
        out_specs=[hbm] * len(out_shape),
        scratch_shapes=scratch
        + [
            pltpu.VMEM((SLOTS, CHUNK, TILE, TILE), F32),
            pltpu.SemaphoreType.DMA((sems,)),
            pltpu.SemaphoreType.DMA((SLOTS,)),
        ],
        cost_estimate=pl.CostEstimate(
            flops=12 * MAXT * TILE * TILE * D, bytes_accessed=60 * 2**20, transcendentals=0
        ),
        compiler_params=pltpu.CompilerParams(vmem_limit_bytes=60 * 2**20),
        name=name,
    )(*scalars, tiles, *panels)


def run_backward(scalars, tiles, cs):
    leaf = jax.ShapeDtypeStruct((4, QUART, D), F32)
    return run_sweep(
        backward_kernel, "backward",
        [jax.ShapeDtypeStruct((16 * NODE, D), F32)] + [leaf] * 4,
        [pltpu.VMEM((8 * BLK, 2 * TILE, D), BF16), pltpu.VMEM((16 * NODE, D), F32)],
        17, scalars, tiles, cs.reshape(8 * BLK, 2 * TILE, D),
    )


def run_forward(scalars, tiles, xs, late):
    return run_sweep(
        forward_kernel, "forward",
        [jax.ShapeDtypeStruct((8 * NODE, D), F32)],
        [
            pltpu.VMEM((16 * BLK, 2 * TILE, D), BF16),
            pltpu.VMEM((8 * NODE, D), F32),
            pltpu.VMEM((4, 4, QUART, D), F32),
        ],
        5, scalars, tiles, xs.reshape(16 * BLK, 2 * TILE, D), *late,
    )[0]


def ring_sends(arrays):
    ways = ((1, 0), (3, 0), (0, 1), (0, 3))
    sent = []
    for array, (dy, dx) in zip(arrays, ways):
        pairs = [(y * 4 + x, (y + dy) % 4 * 4 + (x + dx) % 4) for y in range(4) for x in range(4)]
        sent.append(lax.ppermute(array, "rows", pairs))
    return sent


def scatter_half(net, t, base, leaf, main, leaf2, main2, own_ref, need):
    s, b, slot = row_order(net, base)
    up, down, both = pl.ds(base, QUART), pl.ds(base + QUART, QUART), pl.ds(base, HALF)
    order = SCATTER_TURNS
    b_plus, b_minus = slot(s, b + 1), slot(s, b + 3)
    mains = []
    s_plus, s_minus = slot(s + 1, b), slot(s + 3, b)

    def main_sends(i):
        o = order[i]
        plus, minus = slot(s + o, b + 1), slot(s + o, b + 3)
        need(o, 1)
        need(o, 3)
        t[plus, up] += leaf[0, i]
        t[minus, down] += leaf[1, i]
        return (
            net.send(t.at[plus, both], main.at[i, 0], row=b_plus),
            net.send(t.at[minus, both], main.at[i, 1], row=b_minus),
        )

    def collect(i):
        for copy in mains[i]:
            copy.wait_recv()
        at = slot(s + order[i], b)
        need(order[i], 0)
        t[at, both] += main[i, 0] + main[i, 1]
        return at

    mains.append(main_sends(0))
    yield
    mains.append(main_sends(1))
    yield
    mains.append(main_sends(2))
    yield
    at = collect(0)
    leaves2 = (
        net.send(t.at[at, up], leaf2.at[0], row=s_plus),
        net.send(t.at[at, down], leaf2.at[1], row=s_minus),
    )
    yield
    mains.append(main_sends(3))
    yield
    collect(1)
    yield
    collect(2)
    for copy in leaves2:
        copy.wait_recv()
    t[s_plus, up] += leaf2[0]
    t[s_minus, down] += leaf2[1]
    mains2 = (
        net.send(t.at[s_plus, both], main2.at[0], row=s_plus),
        net.send(t.at[s_minus, both], main2.at[1], row=s_minus),
    )
    yield
    collect(3)
    yield
    for copy in mains2:
        copy.wait_recv()
    own_ref[both, :] = t[slot(s, b), both] + (main2[0] + main2[1])


SCATTER_COPIES = 4 * 2 + 2 + 2


def scatter_cols(net, f_hbm, f, pair, leaf, main, ready):
    z, k = net.z, net.k
    up, down = pl.ds(0, HALF), pl.ds(HALF, HALF)
    order = (2, 1, 3, 0)
    copies = [
        net.send(f_hbm.at[(z + o) % 4 * 2 + 1 - k], pair.at[i], col=z * 2 + 1 - k)
        for i, o in enumerate(order)
    ]
    yield
    plus, minus = (z + 1) % 4 * 2 + k, (z + 3) % 4 * 2 + k
    for i, o in enumerate(order):
        copies[i].wait_recv()
        ready(o)
        at = (z + o) % 4 * 2 + k
        f[at] += pair[i]
        if o == 2:
            leaves = (
                net.send(f.at[at, up], leaf.at[0], col=plus),
                net.send(f.at[at, down], leaf.at[1], col=minus),
            )
            yield
    yield
    for copy in leaves:
        copy.wait_recv()
    f[plus, up] += leaf[0]
    f[minus, down] += leaf[1]
    mains = (
        net.send(f.at[plus], main.at[0], col=plus),
        net.send(f.at[minus], main.at[1], col=minus),
    )
    yield
    for copy in mains:
        copy.wait_recv()
    f[net.c] += main[0] + main[1]


SCATTER_COLS_COPIES = 4 + 2 + 2


SCATTER_ORDER = "gabgtabttggababtabtgababtggabtgabg"


T_ORDER = [(2, 1), (2, 3), (1, 2), (3, 2), (1, 1), (1, 3), (3, 1), (3, 3), (2, 0), (0, 2)]
T_ORDER += [(0, 1), (0, 3), (1, 0), (3, 0), (0, 0), (2, 2)]


def scatter_kernel(
    x_ref, c_ref, wq_ref, wk_ref, wv_ref, wg_ref,
    att_ref, gq_ref, key_ref, val_ref, gs_ref, gks_ref, f_hbm, t_hbm, first0, first1, first2, first3,
    own_ref, out_ref, gx_ref, dq_ref, dk_ref, dv_ref, dg_ref,
    f, t, leaf, main, leaf2, main2, pair, zleaf, zmain, load_sem, ssem, rsem, *reduce_refs,
):
    net = Net(ssem, rsem)
    loads = {}

    def load(key, source, target):
        loads[key] = pltpu.make_async_copy(source, target, load_sem.at[len(loads)])
        loads[key].start()

    for i, first in enumerate((first0, first1, first2, first3)):
        load(i, first, leaf.at[i // 2, i % 2])
    for i, (dx, dy) in enumerate(T_ORDER):
        slot = (net.y + dy) % 4 * 4 + (net.x + dx) % 4
        load((dx, dy), t_hbm.at[slot], t.at[slot])
        if i == 3:
            for o in (2, 1, 3, 0):
                at = (net.z + o) % 4 * 2 + net.k
                load(("f", o), f_hbm.at[at], f.at[at])
    net.barrier()
    ar1, ar2 = reduce_refs[:7], reduce_refs[7:]

    def need(*keys):
        for key in keys:
            if key in loads:
                loads.pop(key).wait()

    def attention():
        for i in range(NODE // CH):
            rows = pl.ds(i * CH, CH)
            x = x_ref[rows, :]
            key = key_ref[rows, :]
            gq = gq_ref[rows, :]
            gk = (dot(val_ref[rows, :], gs_ref[...], NT) + gks_ref[0:1, :]) * slope(key)
            gv = dot(feat(key), gs_ref[...])
            gx = dot(gq, wq_ref[...], NT) + dot(gk, wk_ref[...], NT)
            gx_ref[rows, :] = gx + dot(gv, wv_ref[...], NT)
            for j, grad in enumerate((gq, gk, gv)):
                product = dot(x, grad, TN).reshape(8, 32, D)
                at = pl.ds(32 * j, 32)
                ar1[0][:, at, :] = product if i == 0 else ar1[0][:, at, :] + product
            yield
        yield from all_reduce(net, ar1[0], None, *ar1[2:])
        for j, grad in enumerate((dq_ref, dk_ref, dv_ref)):
            grad[...] = ar1[6][:, pl.ds(32 * j, 32), :].reshape(D, D)

    def graph():
        yield from scatter_cols(net, f_hbm, f, pair, zleaf, zmain, lambda o: need(("f", o)))
        dg_ref[...] = jnp.zeros((D, D), F32)

        @pl.loop(0, NODE // CH)
        def _(i):
            rows = pl.ds(pl.multiple_of(i * CH, CH), CH)
            mixed = f[net.c, rows, :]
            out_ref[rows, :] = att_ref[rows, :] + dot(mixed, wg_ref[...])
            dg_ref[...] += dot(mixed, c_ref[rows, :], TN)

        ar2[0][...] = dg_ref[...].reshape(8, 32, D)
        yield from all_reduce(net, ar2[0], None, *ar2[2:])
        dg_ref[...] = ar2[6][...].reshape(D, D)

    def half(i):
        def wanted(small, big):
            need(0, 1, 2, 3, (small, big) if i == 0 else (big, small))

        return scatter_half(net, t, i * HALF, leaf.at[i], main.at[i], leaf2.at[i], main2.at[i], own_ref, wanted)

    drive(SCATTER_ORDER, a=half(0), b=half(1), g=graph(), t=attention())
    need(*list(loads))
    net.finish()


def run_scatter(x, cot, wq, wk, wv, wg, att, gq, key, val, gs, gks, f, t, firsts):
    copies = 2 * SCATTER_COPIES + SCATTER_COLS_COPIES + 2 * REDUCE_COPIES
    block, weight = jax.ShapeDtypeStruct((NODE, D), F32), jax.ShapeDtypeStruct((D, D), F32)
    vmem, hbm = pl.BlockSpec(memory_space=pltpu.VMEM), pl.BlockSpec(memory_space=pltpu.HBM)
    return pl.pallas_call(
        scatter_kernel,
        out_shape=[block, block, block, weight, weight, weight, weight],
        in_specs=[vmem] * 12 + [hbm] * 6,
        out_specs=[vmem] * 7,
        scratch_shapes=[
            pltpu.VMEM((8, NODE, D), F32),
            pltpu.VMEM((16, NODE, D), F32),
            pltpu.VMEM((2, 2, 4, QUART, D), F32),
            pltpu.VMEM((2, 4, 2, HALF, D), F32),
            pltpu.VMEM((2, 2, QUART, D), F32),
            pltpu.VMEM((2, 2, HALF, D), F32),
            pltpu.VMEM((4, NODE, D), F32),
            pltpu.VMEM((2, HALF, D), F32),
            pltpu.VMEM((2, NODE, D), F32),
            pltpu.SemaphoreType.DMA((24,)),
            pltpu.SemaphoreType.DMA((copies,)),
            pltpu.SemaphoreType.DMA((copies,)),
        ]
        + reduce_scratch(96, 0)
        + reduce_scratch(32, 0),
        compiler_params=pltpu.CompilerParams(
            collective_id=1, has_side_effects=True, vmem_limit_bytes=60 * 2**20
        ),
        name="scatter",
    )(x, cot, wq, wk, wv, wg, att, gq, key, val, gs, gks, f, t, *firsts)


def finish_kernel(own_hbm, wg_ref, *refs):
    taken, given, held, (own, load_sem, store_sem) = refs[:6], refs[6:12], refs[12:18], refs[18:]
    loads = [pltpu.make_async_copy(own_hbm, own, load_sem.at[6])]
    for i in range(6):
        loads.append(pltpu.make_async_copy(taken[i], held[i], load_sem.at[i]))
    for copy in loads:
        copy.start()
    stores = [pltpu.make_async_copy(held[i], given[i], store_sem.at[i]) for i in range(6)]
    loads[0].wait()
    term = dot(own[...], wg_ref[...], NT)
    loads[1].wait()
    held[0][...] += term
    stores[0].start()
    for i in range(1, 6):
        loads[i + 1].wait()
        stores[i].start()
    for copy in stores:
        copy.wait()


def run_finish(own, wg, out, gx, *weights):
    vmem, hbm = pl.BlockSpec(memory_space=pltpu.VMEM), pl.BlockSpec(memory_space=pl.ANY)
    gx, out, *weights = pl.pallas_call(
        finish_kernel,
        out_shape=[jax.ShapeDtypeStruct(a.shape, F32) for a in (gx, out, *weights)],
        in_specs=[hbm, vmem] + [hbm] * 6,
        out_specs=[hbm] * 6,
        scratch_shapes=[
            *[pltpu.VMEM(a.shape, F32) for a in (gx, out, *weights)],
            pltpu.VMEM((NODE, D), F32),
            pltpu.SemaphoreType.DMA((7,)),
            pltpu.SemaphoreType.DMA((6,)),
        ],
        compiler_params=pltpu.CompilerParams(vmem_limit_bytes=60 * 2**20),
        name="finish",
    )(own, wg, gx, out, *weights)
    return (out, gx, *weights)


def per_device(x, cot, wq, wk, wv, wg, tiles, tile_rows, tile_cols, tile_count):
    xs, cs, *rest = run_gather(x, cot, wq, wk, wv)
    last, (att, gq, key, val, gs, gks) = rest[:4], rest[4:]
    row = lax.axis_index("rows")
    scalars = (tile_rows, tile_cols, tile_count, jnp.stack([row // 4, row % 4]))
    late = ring_sends(last)
    t, *leaves = run_backward(scalars, tiles, cs)
    firsts = ring_sends(leaves)
    f = run_forward(scalars, tiles, xs, late).reshape(8, NODE, D)
    t = t.reshape(16, NODE, D)
    own, *results = run_scatter(x, cot, wq, wk, wv, wg, att, gq, key, val, gs, gks, f, t, firsts)
    return run_finish(own, wg, *results)


def solution(mesh):
    nodes = P(("rows", "cols"), None)
    slots = P(("rows", "cols"))
    return jax.shard_map(
        per_device,
        mesh=mesh,
        in_specs=(nodes, nodes, P(), P(), P(), P(), P(("rows", "cols"), None, None), slots, slots, slots),
        out_specs=(nodes, nodes, P(), P(), P(), P()),
        check_vma=False,
    )
```

```python
import jax
import jax.numpy as jnp
from jax import lax
from jax.experimental import pallas as pl
from jax.experimental.pallas import tpu as pltpu
from jax.sharding import PartitionSpec as P

MESH = pl.DeviceIdType.MESH
F32, BF16 = jnp.float32, jnp.bfloat16
TILE, D, NODE, MAXT = 128, 256, 768, 288
HALF, QUART = NODE // 2, NODE // 4
BLK = NODE // TILE
CH = 384
NN, NT, TN = ((1,), (0,)), ((1,), (1,)), ((0,), (0,))


def dot(a, b, dims=NN):
    (a_hi, a_lo), (b_hi, b_lo) = split2(a), split2(b)

    def one(p, q):
        return lax.dot_general(p, q, (dims, ((), ())), preferred_element_type=F32)

    return one(a_hi, b_hi) + (one(a_hi, b_lo) + one(a_lo, b_hi))


def feat(v):
    return jnp.where(v > 0, v + 1.0, jnp.exp(jnp.minimum(v, 0.0)))


def slope(v):
    return jnp.where(v > 0, 1.0, jnp.exp(jnp.minimum(v, 0.0)))


def split2(v):
    hi = v.astype(BF16)
    return hi, (v - hi.astype(F32)).astype(BF16)


class Net:
    def __init__(self, ssem, rsem):
        self.ssem, self.rsem, self.n, self.sent = ssem, rsem, 0, []
        self.r, self.c = lax.axis_index("rows"), lax.axis_index("cols")
        self.y, self.x = self.r // 4, self.r % 4
        self.z, self.k = self.c // 2, self.c % 2

    def send(self, src, dst, row=None, col=None):
        i, self.n = self.n, self.n + 1
        copy = pltpu.make_async_remote_copy(
            src_ref=src,
            dst_ref=dst,
            send_sem=self.ssem.at[i],
            recv_sem=self.rsem.at[i],
            device_id=(self.r if row is None else row, self.c if col is None else col),
            device_id_type=MESH,
        )
        copy.start()
        self.sent.append(copy)
        return copy

    def barrier(self):
        sem = pltpu.get_barrier_semaphore()
        there = [(self.r, (self.c + j) % 8) for j in range(1, 8)]
        there += [(self.y * 4 + (self.x + j) % 4, self.c) for j in range(1, 4)]
        there += [((self.y + j) % 4 * 4 + self.x, self.c) for j in range(1, 4)]
        for device in there:
            pl.semaphore_signal(sem, inc=1, device_id=device, device_id_type=MESH)
        pl.semaphore_wait(sem, len(there))

    def finish(self):
        for copy in self.sent:
            copy.wait_send()


def all_reduce(net, part, key, r0, r1, kbuf, r2, r3, full):
    x, y, z, k = net.x, net.y, net.z, net.k
    n = part.shape[1]
    sibling = z * 2 + 1 - k
    mine, theirs = pl.ds(k * 4, 4), pl.ds((1 - k) * 4, 4)
    first = [net.send(part.at[theirs], r0, col=sibling)]
    if key is not None:
        kbuf[4] = key[...]
        first.append(net.send(kbuf.at[4], kbuf.at[3], col=sibling))
    for copy in first:
        copy.wait_recv()
    part[mine] += r0[...]
    if key is not None:
        key[...] += kbuf[3]
    first = []
    for j in range(1, 4):
        to = (z + j) % 4
        first.append(net.send(part.at[k * 4 + to], r1.at[j - 1], col=to * 2 + k))
        if key is not None:
            first.append(net.send(key, kbuf.at[j - 1], col=to * 2 + k))
    yield
    for copy in first:
        copy.wait_recv()
    r2[x, 0:n] = (part[k * 4 + z] + r1[0]) + (r1[1] + r1[2])
    if key is not None:
        r2[x, n:] = (key[...] + kbuf[0]) + (kbuf[1] + kbuf[2])
    second = [net.send(r2.at[x], r2.at[x], row=y * 4 + (x + j) % 4) for j in range(1, 4)]
    yield
    for copy in second:
        copy.wait_recv()
    r3[y] = (r2[0] + r2[1]) + (r2[2] + r2[3])
    third = [net.send(r3.at[y], r3.at[y], row=(y + j) % 4 * 4 + x) for j in range(1, 4)]
    yield
    for copy in third:
        copy.wait_recv()
    at = k * 4 + z
    full[at] = (r3[0, 0:n] + r3[1, 0:n]) + (r3[2, 0:n] + r3[3, 0:n])
    fourth = [net.send(full.at[at], full.at[at], col=(z + j) % 4 * 2 + k) for j in range(1, 4)]
    yield
    for copy in fourth:
        copy.wait_recv()
    net.send(full.at[mine], full.at[mine], col=sibling).wait_recv()


def key_total(r3, n):
    return (r3[0, n:] + r3[1, n:]) + (r3[2, n:] + r3[3, n:])


def reduce_scratch(n, extra):
    return [
        pltpu.VMEM((8, n, D), F32),
        pltpu.VMEM((8, D), F32),
        pltpu.VMEM((4, n, D), F32),
        pltpu.VMEM((3, n, D), F32),
        pltpu.VMEM((5, 8, D), F32),
        pltpu.VMEM((4, n + extra, D), F32),
        pltpu.VMEM((4, n + extra, D), F32),
        pltpu.VMEM((8, n, D), F32),
    ]


REDUCE_COPIES = 2 + 6 + 3 + 3 + 3 + 1


def row_order(net, base):
    if base == 0:
        return net.x, net.y, lambda first, then: then % 4 * 4 + first % 4
    return net.y, net.x, lambda first, then: first % 4 * 4 + then % 4


def gather_half(net, mine, panel, base, done, keep):
    a, b, slot = row_order(net, base)
    all_rows, up, down = pl.ds(base, HALF), pl.ds(base, QUART), pl.ds(base + QUART, QUART)

    def pair(src, at, rows, plus, minus):
        view = panel.at[at, rows]
        source = view if src is None else src.at[rows]
        return net.send(source, view, row=plus), net.send(source, view, row=minus)

    def forward(at, rows, row):
        return net.send(panel.at[at, rows], panel.at[at, rows], row=row)

    own = slot(a, b)
    a_plus, a_minus = slot(a + 1, b), slot(a - 1 + 4, b)
    b_plus, b_minus = slot(a, b + 1), slot(a, b - 1 + 4)
    from_left, from_right = pair(mine, own, all_rows, a_plus, a_minus)
    yield
    second = {0: pair(mine, own, all_rows, b_plus, b_minus)}
    yield
    from_left.wait_recv()
    fwd_up = forward(slot(a + 3, b), up, a_plus)
    second[3] = pair(None, slot(a + 3, b), all_rows, b_plus, b_minus)
    from_right.wait_recv()
    fwd_down = forward(slot(a + 1, b), down, a_minus)
    yield
    second[1] = pair(None, slot(a + 1, b), all_rows, b_plus, b_minus)
    done(3, 0)
    done(1, 0)

    def pass_on(o):
        left, right = second[o]
        left.wait_recv()
        keep(0, o, panel.at[slot(a + o, b + 3), up])
        right.wait_recv()
        keep(1, o, panel.at[slot(a + o, b + 1), down])
        done(o, 3)
        done(o, 1)

    yield
    pass_on(0)
    yield
    fwd_up.wait_recv()
    fwd_down.wait_recv()
    second[2] = pair(None, slot(a + 2, b), all_rows, b_plus, b_minus)
    done(2, 0)
    yield
    pass_on(3)
    yield
    pass_on(1)
    yield
    pass_on(2)


GATHER_COPIES = 2 + 2 + 4 * 2


def gather_cols(net, mine, panel, done):
    z, k = net.z, net.k
    own = net.c
    plus, minus = (z + 1) % 4 * 2 + k, (z + 3) % 4 * 2 + k
    opposite = (z + 2) % 4 * 2 + k
    sibling = z * 2 + 1 - k
    up, down = pl.ds(0, HALF), pl.ds(HALF, HALF)
    left = net.send(mine, panel.at[own], col=plus)
    right = net.send(mine, panel.at[own], col=minus)
    pair = [net.send(mine, panel.at[own], col=sibling)]
    yield
    left.wait_recv()
    f_up = net.send(panel.at[minus, up], panel.at[minus, up], col=plus)
    pair.append(net.send(panel.at[minus], panel.at[minus], col=sibling))
    right.wait_recv()
    f_down = net.send(panel.at[plus, down], panel.at[plus, down], col=minus)
    pair.append(net.send(panel.at[plus], panel.at[plus], col=sibling))
    done(minus)
    done(plus)
    yield
    f_up.wait_recv()
    f_down.wait_recv()
    pair.append(net.send(panel.at[opposite], panel.at[opposite], col=sibling))
    done(opposite)
    yield
    for o, copy in zip((0, 3, 1, 2), pair):
        copy.wait_recv()
        done((z + o) % 4 * 2 + 1 - k)
    yield


COLS_COPIES = 3 + 4 + 1


def drive(order, **runs):
    def step(name):
        try:
            next(runs[name])
        except StopIteration:
            del runs[name]

    for name in order:
        if name in runs:
            step(name)
    while runs:
        for name in list(runs):
            step(name)


GATHER_ORDER = "abtctabotabtabtctbtaababctabctabtab"


def gather_kernel(
    x_ref, c_ref, wq_ref, wk_ref, wv_ref,
    xs_ref, cs_ref, last0, last1, last2, last3, att_out, gq_out, key_out, val_out, gs_ref, gks_ref,
    att_ref, gq_ref, key_ref, val_ref, q_ref, xp, cp, x_stage, c_stage, stage_sem, ssem, rsem, *reduce_refs,
):
    net = Net(ssem, rsem)
    net.barrier()
    last_refs = (last0, last1, last2, last3)
    ar1, ar2 = reduce_refs[:8], reduce_refs[8:]
    staged = []

    def send_out(source, target):
        copy = pltpu.make_async_copy(source, target, stage_sem.at[len(staged)])
        copy.start()
        staged.append(copy)

    def split_out(source, stage, out, slot, first=0, blocks=BLK):
        @pl.loop(first, first + blocks)
        def _(i):
            hi, lo = split2(source[pl.ds(pl.multiple_of(i * TILE, TILE), TILE), :])
            stage[slot, i, 0:TILE, :] = hi
            stage[slot, i, TILE : 2 * TILE, :] = lo

        at = pl.ds(first, blocks)
        send_out(stage.at[slot, at], out.at[slot, at])

    def x_done(half, dx, dy):
        slot = (net.y + dy) % 4 * 4 + (net.x + dx) % 4
        split_out(xp.at[slot], x_stage, xs_ref, slot, half * BLK // 2, BLK // 2)

    def keep(half):
        return lambda way, o, source: send_out(source, last_refs[2 * half + way].at[o])

    def cols_done(slot):
        split_out(cp.at[slot], c_stage, cs_ref, slot)

    def attention():
        def first(i, sums):
            state, key_sum = sums
            rows = pl.ds(pl.multiple_of(i * CH, CH), CH)
            x = x_ref[rows, :]
            q_ref[rows, :] = dot(x, wq_ref[...])
            key = dot(x, wk_ref[...])
            val = dot(x, wv_ref[...])
            key_ref[rows, :] = key
            val_ref[rows, :] = val
            feat_k = feat(key)
            return state + dot(feat_k, val, TN), key_sum + jnp.sum(feat_k, axis=0, keepdims=True)

        zero = (jnp.zeros((D, D), F32), jnp.zeros((1, D), F32))
        state, key_sum = lax.fori_loop(0, NODE // CH, first, zero)
        send_out(key_ref, key_out)
        send_out(val_ref, val_out)
        ar1[0][...] = state.reshape(8, 32, D)
        ar1[1][...] = jnp.broadcast_to(key_sum, (8, D))
        yield from all_reduce(net, *ar1)
        state = ar1[7][...].reshape(D, D)
        key_row = key_total(ar1[6], 32)[0:1]

        def second(i, sums):
            grad_state, grad_key_sum = sums
            rows = pl.ds(pl.multiple_of(i * CH, CH), CH)
            q = q_ref[rows, :]
            cot = c_ref[rows, :]
            feat_q = feat(q)
            den = jnp.sum(feat_q * key_row, axis=1, keepdims=True)
            att = dot(feat_q, state) / den
            att_ref[rows, :] = att
            scaled = cot / den
            weight_dot = jnp.sum(cot * att, axis=1, keepdims=True) / den
            gq_ref[rows, :] = (dot(scaled, state, NT) - weight_dot * key_row) * slope(q)
            return (
                grad_state + dot(feat_q, scaled, TN),
                grad_key_sum - jnp.sum(feat_q * weight_dot, axis=0, keepdims=True),
            )

        grad_state, grad_key_sum = lax.fori_loop(0, NODE // CH, second, zero)
        send_out(att_ref, att_out)
        send_out(gq_ref, gq_out)
        ar2[0][...] = grad_state.reshape(8, 32, D)
        ar2[1][...] = jnp.broadcast_to(grad_key_sum, (8, D))
        yield from all_reduce(net, *ar2)
        gs_ref[...] = ar2[7][...].reshape(D, D)
        gks_ref[...] = key_total(ar2[6], 32)

    def own_blocks():
        yield
        split_out(x_ref, x_stage, xs_ref, net.r)
        split_out(c_ref, c_stage, cs_ref, net.c)

    drive(
        GATHER_ORDER,
        a=gather_half(net, x_ref, xp, 0, lambda dx, dy: x_done(0, dx, dy), keep(0)),
        b=gather_half(net, x_ref, xp, HALF, lambda dy, dx: x_done(1, dx, dy), keep(1)),
        c=gather_cols(net, c_ref, cp, cols_done),
        t=attention(),
        o=own_blocks(),
    )
    net.finish()
    for copy in staged:
        copy.wait()


def run_gather(x, cot, wq, wk, wv):
    copies = 2 * GATHER_COPIES + COLS_COPIES + 2 * REDUCE_COPIES
    block = jax.ShapeDtypeStruct((NODE, D), F32)
    vmem, hbm = pl.BlockSpec(memory_space=pltpu.VMEM), pl.BlockSpec(memory_space=pl.ANY)
    return pl.pallas_call(
        gather_kernel,
        out_shape=[
            jax.ShapeDtypeStruct((16, BLK, 2 * TILE, D), BF16),
            jax.ShapeDtypeStruct((8, BLK, 2 * TILE, D), BF16),
            *[jax.ShapeDtypeStruct((4, QUART, D), F32)] * 4,
            block, block, block, block,
            jax.ShapeDtypeStruct((D, D), F32),
            jax.ShapeDtypeStruct((8, D), F32),
        ],
        in_specs=[vmem] * 5,
        out_specs=[hbm] * 10 + [vmem] * 2,
        scratch_shapes=[
            *[pltpu.VMEM((NODE, D), F32)] * 5,
            pltpu.VMEM((16, NODE, D), F32),
            pltpu.VMEM((8, NODE, D), F32),
            pltpu.VMEM((16, BLK, 2 * TILE, D), BF16),
            pltpu.VMEM((8, BLK, 2 * TILE, D), BF16),
            pltpu.SemaphoreType.DMA((2 * 11 + 16 + 9 + 4,)),
            pltpu.SemaphoreType.DMA((copies,)),
            pltpu.SemaphoreType.DMA((copies,)),
        ]
        + reduce_scratch(32, 8)
        + reduce_scratch(32, 8),
        compiler_params=pltpu.CompilerParams(
            collective_id=0, has_side_effects=True, vmem_limit_bytes=60 * 2**20
        ),
        name="gather",
    )(x, cot, wq, wk, wv)


CHUNK = 32
SLOTS = 3


def sweep(count, rows_ref, cols_ref, tiles_ref, buf, tile_sem, body):
    chunks = (count + CHUNK - 1) // CHUNK

    def fetch(chunk, slot):
        return pltpu.make_async_copy(
            tiles_ref.at[pl.ds(chunk * CHUNK, CHUNK)], buf.at[slot], tile_sem.at[slot]
        )

    for i in range(SLOTS - 1):
        @pl.when(i < chunks)
        def _(i=i):
            fetch(i, i).start()

    @pl.loop(0, chunks)
    def _(chunk):
        slot = chunk % SLOTS

        @pl.when(chunk + SLOTS - 1 < chunks)
        def _():
            fetch(chunk + SLOTS - 1, (chunk + SLOTS - 1) % SLOTS).start()

        fetch(chunk, slot).wait()
        for i in range(CHUNK):
            at = chunk * CHUNK + i
            tile = buf[slot, i]
            body(jnp.where(at < count, tile, 0.0), rows_ref[at], cols_ref[at])


def product(tile, panel):
    hi, lo = split2(tile)
    whole = jnp.dot(jnp.concatenate([hi, hi], axis=1), panel, preferred_element_type=F32)
    return whole + jnp.dot(lo, panel[0:TILE], preferred_element_type=F32)


def block_rows(block):
    return pl.ds(pl.multiple_of(block * TILE, TILE), TILE)


def backward_kernel(
    rows_ref, cols_ref, count_ref, place_ref, tiles_ref, cs_ref,
    t_ref, leaf0, leaf1, leaf2, leaf3,
    cs, t, buf, sem, tile_sem,
):
    load = pltpu.make_async_copy(cs_ref, cs, sem.at[0])
    load.start()
    t[...] = jnp.zeros_like(t)
    load.wait()

    def body(tile, row, col):
        t[block_rows(col), :] += product(tile.T, cs[row])

    sweep(count_ref[0], rows_ref, cols_ref, tiles_ref, buf, tile_sem, body)
    y, x = place_ref[0], place_ref[1]
    stores = [pltpu.make_async_copy(t, t_ref, sem.at[0])]
    for kind, leaf in enumerate((leaf0, leaf1, leaf2, leaf3)):
        for i, o in enumerate(SCATTER_TURNS):
            dx, dy = (o, 2) if kind < 2 else (2, o)
            slot = (y + dy) % 4 * 4 + (x + dx) % 4
            source = t.at[pl.ds(pl.multiple_of(slot * NODE + kind * QUART, QUART), QUART)]
            stores.append(pltpu.make_async_copy(source, leaf.at[i], sem.at[1 + 4 * kind + i]))
    for copy in stores:
        copy.start()
    for copy in stores:
        copy.wait()


def forward_kernel(
    rows_ref, cols_ref, count_ref, place_ref, tiles_ref, xs_ref, last0, last1, last2, last3,
    f_ref,
    xs, f, late, buf, sem, tile_sem,
):
    load = pltpu.make_async_copy(xs_ref, xs, sem.at[0])
    loads = [
        pltpu.make_async_copy(last, late.at[kind], sem.at[1 + kind])
        for kind, last in enumerate((last0, last1, last2, last3))
    ]
    for copy in loads + [load]:
        copy.start()
    f[...] = jnp.zeros_like(f)
    for copy in loads + [load]:
        copy.wait()
    y, x = place_ref[0], place_ref[1]
    for kind in range(4):
        for o in range(4):
            dx, dy = (o, 2) if kind < 2 else (2, o)
            slot = (y + dy) % 4 * 4 + (x + dx) % 4
            for part in range(0, QUART, PART):
                block, at = divmod(kind * QUART + part, TILE)
                hi, lo = split2(late[kind, o, part : part + PART, :])
                xs[slot * BLK + block, at : at + PART, :] = hi
                xs[slot * BLK + block, TILE + at : TILE + at + PART, :] = lo

    def body(tile, row, col):
        f[block_rows(row), :] += product(tile, xs[col])

    sweep(count_ref[0], rows_ref, cols_ref, tiles_ref, buf, tile_sem, body)
    store = pltpu.make_async_copy(f, f_ref, sem.at[0])
    store.start()
    store.wait()


PART = 64
SCATTER_TURNS = (2, 1, 3, 0)


def run_sweep(kernel, name, out_shape, scratch, sems, scalars, tiles, *panels):
    hbm, smem = pl.BlockSpec(memory_space=pltpu.HBM), pl.BlockSpec(memory_space=pltpu.SMEM)
    return pl.pallas_call(
        kernel,
        out_shape=out_shape,
        in_specs=[smem] * 4 + [hbm] * (1 + len(panels)),
        out_specs=[hbm] * len(out_shape),
        scratch_shapes=scratch
        + [
            pltpu.VMEM((SLOTS, CHUNK, TILE, TILE), F32),
            pltpu.SemaphoreType.DMA((sems,)),
            pltpu.SemaphoreType.DMA((SLOTS,)),
        ],
        cost_estimate=pl.CostEstimate(
            flops=12 * MAXT * TILE * TILE * D, bytes_accessed=60 * 2**20, transcendentals=0
        ),
        compiler_params=pltpu.CompilerParams(vmem_limit_bytes=63 * 2**20),
        name=name,
    )(*scalars, tiles, *panels)


def run_backward(scalars, tiles, cs):
    leaf = jax.ShapeDtypeStruct((4, QUART, D), F32)
    return run_sweep(
        backward_kernel, "backward",
        [jax.ShapeDtypeStruct((16 * NODE, D), F32)] + [leaf] * 4,
        [pltpu.VMEM((8 * BLK, 2 * TILE, D), BF16), pltpu.VMEM((16 * NODE, D), F32)],
        17, scalars, tiles, cs.reshape(8 * BLK, 2 * TILE, D),
    )


def run_forward(scalars, tiles, xs, late):
    return run_sweep(
        forward_kernel, "forward",
        [jax.ShapeDtypeStruct((8 * NODE, D), F32)],
        [
            pltpu.VMEM((16 * BLK, 2 * TILE, D), BF16),
            pltpu.VMEM((8 * NODE, D), F32),
            pltpu.VMEM((4, 4, QUART, D), F32),
        ],
        5, scalars, tiles, xs.reshape(16 * BLK, 2 * TILE, D), *late,
    )[0]


def ring_sends(arrays):
    ways = ((1, 0), (3, 0), (0, 1), (0, 3))
    sent = []
    for array, (dy, dx) in zip(arrays, ways):
        pairs = [(y * 4 + x, (y + dy) % 4 * 4 + (x + dx) % 4) for y in range(4) for x in range(4)]
        sent.append(lax.ppermute(array, "rows", pairs))
    return sent


def scatter_half(net, t, base, leaf, main, leaf2, main2, own_ref, need):
    s, b, slot = row_order(net, base)
    up, down, both = pl.ds(base, QUART), pl.ds(base + QUART, QUART), pl.ds(base, HALF)
    order = SCATTER_TURNS
    b_plus, b_minus = slot(s, b + 1), slot(s, b + 3)
    mains = []
    s_plus, s_minus = slot(s + 1, b), slot(s + 3, b)

    def main_sends(i):
        o = order[i]
        plus, minus = slot(s + o, b + 1), slot(s + o, b + 3)
        need(o, 1)
        need(o, 3)
        t[plus, up] += leaf[0, i]
        t[minus, down] += leaf[1, i]
        return (
            net.send(t.at[plus, both], main.at[i, 0], row=b_plus),
            net.send(t.at[minus, both], main.at[i, 1], row=b_minus),
        )

    def collect(i):
        for copy in mains[i]:
            copy.wait_recv()
        at = slot(s + order[i], b)
        need(order[i], 0)
        t[at, both] += main[i, 0] + main[i, 1]
        return at

    mains.append(main_sends(0))
    yield
    mains.append(main_sends(1))
    yield
    mains.append(main_sends(2))
    yield
    at = collect(0)
    leaves2 = (
        net.send(t.at[at, up], leaf2.at[0], row=s_plus),
        net.send(t.at[at, down], leaf2.at[1], row=s_minus),
    )
    yield
    mains.append(main_sends(3))
    yield
    collect(1)
    yield
    collect(2)
    for copy in leaves2:
        copy.wait_recv()
    t[s_plus, up] += leaf2[0]
    t[s_minus, down] += leaf2[1]
    mains2 = (
        net.send(t.at[s_plus, both], main2.at[0], row=s_plus),
        net.send(t.at[s_minus, both], main2.at[1], row=s_minus),
    )
    yield
    collect(3)
    yield
    for copy in mains2:
        copy.wait_recv()
    own_ref[both, :] = t[slot(s, b), both] + (main2[0] + main2[1])


SCATTER_COPIES = 4 * 2 + 2 + 2


def scatter_cols(net, f_hbm, f, pair, leaf, main, ready):
    z, k = net.z, net.k
    up, down = pl.ds(0, HALF), pl.ds(HALF, HALF)
    order = (2, 1, 3, 0)
    copies = [
        net.send(f_hbm.at[(z + o) % 4 * 2 + 1 - k], pair.at[i], col=z * 2 + 1 - k)
        for i, o in enumerate(order)
    ]
    yield
    plus, minus = (z + 1) % 4 * 2 + k, (z + 3) % 4 * 2 + k
    for i, o in enumerate(order):
        copies[i].wait_recv()
        ready(o)
        at = (z + o) % 4 * 2 + k
        f[at] += pair[i]
        if o == 2:
            leaves = (
                net.send(f.at[at, up], leaf.at[0], col=plus),
                net.send(f.at[at, down], leaf.at[1], col=minus),
            )
            yield
    yield
    for copy in leaves:
        copy.wait_recv()
    f[plus, up] += leaf[0]
    f[minus, down] += leaf[1]
    mains = (
        net.send(f.at[plus], main.at[0], col=plus),
        net.send(f.at[minus], main.at[1], col=minus),
    )
    yield
    for copy in mains:
        copy.wait_recv()
    f[net.c] += main[0] + main[1]


SCATTER_COLS_COPIES = 4 + 2 + 2


SCATTER_ORDER = "gabgabtgabttgabtabgtabgabtgabgtg"


T_ORDER = [(2, 1), (2, 3), (1, 2), (3, 2), (1, 1), (1, 3), (3, 1), (3, 3), (2, 0), (0, 2)]
T_ORDER += [(0, 1), (0, 3), (1, 0), (3, 0), (0, 0), (2, 2)]


def scatter_kernel(
    x_in, c_in, wq_ref, wk_ref, wv_ref, wg_ref,
    att_in, gq_in, key_in, val_in, gs_ref, gks_ref, f_hbm, t_hbm, first0, first1, first2, first3,
    own_ref, out_hbm, gx_hbm, dq_ref, dk_ref, dv_ref, dg_ref,
    x_ref, c_ref, att_ref, gq_ref, key_ref, val_ref, out_ref, gx_ref, store_sem,
    f, t, leaf, main, leaf2, main2, pair, zleaf, zmain, load_sem, ssem, rsem, *reduce_refs,
):
    net = Net(ssem, rsem)
    loads = {}

    def load(key, source, target):
        loads[key] = pltpu.make_async_copy(source, target, load_sem.at[len(loads)])
        loads[key].start()

    for i, first in enumerate((first0, first1, first2, first3)):
        load(i, first, leaf.at[i // 2, i % 2])
    for i, (dx, dy) in enumerate(T_ORDER):
        slot = (net.y + dy) % 4 * 4 + (net.x + dx) % 4
        load((dx, dy), t_hbm.at[slot], t.at[slot])
        if i == 3:
            for o in (2, 1, 3, 0):
                at = (net.z + o) % 4 * 2 + net.k
                load(("f", o), f_hbm.at[at], f.at[at])
            load("gq", gq_in, gq_ref)
            load("key", key_in, key_ref)
            load("val", val_in, val_ref)
            load("x", x_in, x_ref)
    load("cot", c_in, c_ref)
    load("att", att_in, att_ref)
    stores = [
        pltpu.make_async_copy(gx_ref, gx_hbm, store_sem.at[0]),
        pltpu.make_async_copy(out_ref, out_hbm, store_sem.at[1]),
    ]
    net.barrier()
    ar1, ar2 = reduce_refs[:8], reduce_refs[8:]

    def need(*keys):
        for key in keys:
            if key in loads:
                loads.pop(key).wait()

    def attention():
        need("gq", "key", "val", "x")
        for i in range(NODE // CH):
            rows = pl.ds(i * CH, CH)
            x = x_ref[rows, :]
            key = key_ref[rows, :]
            gq = gq_ref[rows, :]
            gk = (dot(val_ref[rows, :], gs_ref[...], NT) + gks_ref[0:1, :]) * slope(key)
            gv = dot(feat(key), gs_ref[...])
            gx = dot(gq, wq_ref[...], NT) + dot(gk, wk_ref[...], NT)
            gx_ref[rows, :] = gx + dot(gv, wv_ref[...], NT)
            for j, grad in enumerate((gq, gk, gv)):
                product = dot(x, grad, TN).reshape(8, 32, D)
                at = pl.ds(32 * j, 32)
                ar1[0][:, at, :] = product if i == 0 else ar1[0][:, at, :] + product
            yield
        stores[0].start()
        yield from all_reduce(net, ar1[0], None, *ar1[2:])
        for j, grad in enumerate((dq_ref, dk_ref, dv_ref)):
            grad[...] = ar1[7][:, pl.ds(32 * j, 32), :].reshape(D, D)

    def graph():
        yield from scatter_cols(net, f_hbm, f, pair, zleaf, zmain, lambda o: need(("f", o)))
        dg_ref[...] = jnp.zeros((D, D), F32)
        need("cot", "att")

        @pl.loop(0, NODE // CH)
        def _(i):
            rows = pl.ds(pl.multiple_of(i * CH, CH), CH)
            mixed = f[net.c, rows, :]
            out_ref[rows, :] = att_ref[rows, :] + dot(mixed, wg_ref[...])
            dg_ref[...] += dot(mixed, c_ref[rows, :], TN)

        stores[1].start()
        ar2[0][...] = dg_ref[...].reshape(8, 32, D)
        yield from all_reduce(net, ar2[0], None, *ar2[2:])
        dg_ref[...] = ar2[7][...].reshape(D, D)

    def half(i):
        def wanted(small, big):
            need(0, 1, 2, 3, (small, big) if i == 0 else (big, small))

        return scatter_half(net, t, i * HALF, leaf.at[i], main.at[i], leaf2.at[i], main2.at[i], own_ref, wanted)

    drive(SCATTER_ORDER, a=half(0), b=half(1), g=graph(), t=attention())
    need(*list(loads))
    for copy in stores:
        copy.wait()
    net.finish()


def run_scatter(x, cot, wq, wk, wv, wg, att, gq, key, val, gs, gks, f, t, firsts):
    copies = 2 * SCATTER_COPIES + SCATTER_COLS_COPIES + 2 * REDUCE_COPIES
    block, weight = jax.ShapeDtypeStruct((NODE, D), F32), jax.ShapeDtypeStruct((D, D), F32)
    vmem, hbm = pl.BlockSpec(memory_space=pltpu.VMEM), pl.BlockSpec(memory_space=pltpu.HBM)
    return pl.pallas_call(
        scatter_kernel,
        out_shape=[block, block, block, weight, weight, weight, weight],
        in_specs=[hbm] * 2 + [vmem] * 4 + [hbm] * 4 + [vmem] * 2 + [hbm] * 6,
        out_specs=[vmem] + [hbm] * 2 + [vmem] * 4,
        scratch_shapes=[
            *[pltpu.VMEM((NODE, D), F32)] * 8,
            pltpu.SemaphoreType.DMA((2,)),
            pltpu.VMEM((8, NODE, D), F32),
            pltpu.VMEM((16, NODE, D), F32),
            pltpu.VMEM((2, 2, 4, QUART, D), F32),
            pltpu.VMEM((2, 4, 2, HALF, D), F32),
            pltpu.VMEM((2, 2, QUART, D), F32),
            pltpu.VMEM((2, 2, HALF, D), F32),
            pltpu.VMEM((4, NODE, D), F32),
            pltpu.VMEM((2, HALF, D), F32),
            pltpu.VMEM((2, NODE, D), F32),
            pltpu.SemaphoreType.DMA((30,)),
            pltpu.SemaphoreType.DMA((copies,)),
            pltpu.SemaphoreType.DMA((copies,)),
        ]
        + reduce_scratch(96, 0)
        + reduce_scratch(32, 0),
        compiler_params=pltpu.CompilerParams(
            collective_id=1, has_side_effects=True, vmem_limit_bytes=60 * 2**20
        ),
        name="scatter",
    )(x, cot, wq, wk, wv, wg, att, gq, key, val, gs, gks, f, t, *firsts)


def finish_kernel(own_hbm, wg_ref, *refs):
    taken, given, held, (own, load_sem, store_sem) = refs[:6], refs[6:12], refs[12:18], refs[18:]
    loads = [pltpu.make_async_copy(own_hbm, own, load_sem.at[6])]
    for i in range(6):
        loads.append(pltpu.make_async_copy(taken[i], held[i], load_sem.at[i]))
    for copy in loads:
        copy.start()
    stores = [pltpu.make_async_copy(held[i], given[i], store_sem.at[i]) for i in range(6)]
    loads[0].wait()
    term = dot(own[...], wg_ref[...], NT)
    loads[1].wait()
    held[0][...] += term
    stores[0].start()
    for i in range(1, 6):
        loads[i + 1].wait()
        stores[i].start()
    for copy in stores:
        copy.wait()


def run_finish(own, wg, out, gx, *weights):
    vmem, hbm = pl.BlockSpec(memory_space=pltpu.VMEM), pl.BlockSpec(memory_space=pl.ANY)
    gx, out, *weights = pl.pallas_call(
        finish_kernel,
        out_shape=[jax.ShapeDtypeStruct(a.shape, F32) for a in (gx, out, *weights)],
        in_specs=[hbm, vmem] + [hbm] * 6,
        out_specs=[hbm] * 6,
        scratch_shapes=[
            *[pltpu.VMEM(a.shape, F32) for a in (gx, out, *weights)],
            pltpu.VMEM((NODE, D), F32),
            pltpu.SemaphoreType.DMA((7,)),
            pltpu.SemaphoreType.DMA((6,)),
        ],
        compiler_params=pltpu.CompilerParams(vmem_limit_bytes=60 * 2**20),
        name="finish",
    )(own, wg, gx, out, *weights)
    return (out, gx, *weights)


def per_device(x, cot, wq, wk, wv, wg, tiles, tile_rows, tile_cols, tile_count):
    xs, cs, *rest = run_gather(x, cot, wq, wk, wv)
    last, (att, gq, key, val, gs, gks) = rest[:4], rest[4:]
    row = lax.axis_index("rows")
    scalars = (tile_rows, tile_cols, tile_count, jnp.stack([row // 4, row % 4]))
    late = ring_sends(last)
    t, *leaves = run_backward(scalars, tiles, cs)
    firsts = ring_sends(leaves)
    f = run_forward(scalars, tiles, xs, late).reshape(8, NODE, D)
    t = t.reshape(16, NODE, D)
    own, *results = run_scatter(x, cot, wq, wk, wv, wg, att, gq, key, val, gs, gks, f, t, firsts)
    return run_finish(own, wg, *results)


def solution(mesh):
    nodes = P(("rows", "cols"), None)
    slots = P(("rows", "cols"))
    return jax.shard_map(
        per_device,
        mesh=mesh,
        in_specs=(nodes, nodes, P(), P(), P(), P(), P(("rows", "cols"), None, None), slots, slots, slots),
        out_specs=(nodes, nodes, P(), P(), P(), P()),
        check_vma=False,
    )
```

```python
import jax
import jax.numpy as jnp
from jax import lax
from jax.experimental import pallas as pl
from jax.experimental.pallas import tpu as pltpu
from jax.sharding import PartitionSpec as P

MESH = pl.DeviceIdType.MESH
F32, BF16 = jnp.float32, jnp.bfloat16
TILE, D, NODE, MAXT = 128, 256, 768, 288
HALF, QUART = NODE // 2, NODE // 4
BLK = NODE // TILE
CH = 384
NN, NT, TN = ((1,), (0,)), ((1,), (1,)), ((0,), (0,))


def dot(a, b, dims=NN):
    (a_hi, a_lo), (b_hi, b_lo) = split2(a), split2(b)

    def one(p, q):
        return lax.dot_general(p, q, (dims, ((), ())), preferred_element_type=F32)

    return one(a_hi, b_hi) + (one(a_hi, b_lo) + one(a_lo, b_hi))


def feat(v):
    return jnp.where(v > 0, v + 1.0, jnp.exp(jnp.minimum(v, 0.0)))


def slope(v):
    return jnp.where(v > 0, 1.0, jnp.exp(jnp.minimum(v, 0.0)))


def split2(v):
    hi = v.astype(BF16)
    return hi, (v - hi.astype(F32)).astype(BF16)


class Net:
    def __init__(self, ssem, rsem):
        self.ssem, self.rsem, self.n, self.sent = ssem, rsem, 0, []
        self.r, self.c = lax.axis_index("rows"), lax.axis_index("cols")
        self.y, self.x = self.r // 4, self.r % 4
        self.z, self.k = self.c // 2, self.c % 2

    def send(self, src, dst, row=None, col=None):
        i, self.n = self.n, self.n + 1
        copy = pltpu.make_async_remote_copy(
            src_ref=src,
            dst_ref=dst,
            send_sem=self.ssem.at[i],
            recv_sem=self.rsem.at[i],
            device_id=(self.r if row is None else row, self.c if col is None else col),
            device_id_type=MESH,
        )
        copy.start()
        self.sent.append(copy)
        return copy

    def barrier(self):
        sem = pltpu.get_barrier_semaphore()
        there = [(self.r, (self.c + j) % 8) for j in range(1, 8)]
        there += [(self.y * 4 + (self.x + j) % 4, self.c) for j in range(1, 4)]
        there += [((self.y + j) % 4 * 4 + self.x, self.c) for j in range(1, 4)]
        for device in there:
            pl.semaphore_signal(sem, inc=1, device_id=device, device_id_type=MESH)
        pl.semaphore_wait(sem, len(there))

    def finish(self):
        for copy in self.sent:
            copy.wait_send()


def all_reduce(net, part, key, r0, r1, kbuf, r2, r3, full):
    x, y, z, k = net.x, net.y, net.z, net.k
    n = part.shape[1]
    sibling = z * 2 + 1 - k
    mine, theirs = pl.ds(k * 4, 4), pl.ds((1 - k) * 4, 4)
    first = [net.send(part.at[theirs], r0, col=sibling)]
    if key is not None:
        kbuf[4] = key[...]
        first.append(net.send(kbuf.at[4], kbuf.at[3], col=sibling))
    for copy in first:
        copy.wait_recv()
    part[mine] += r0[...]
    if key is not None:
        key[...] += kbuf[3]
    first = []
    for j in range(1, 4):
        to = (z + j) % 4
        first.append(net.send(part.at[k * 4 + to], r1.at[j - 1], col=to * 2 + k))
        if key is not None:
            first.append(net.send(key, kbuf.at[j - 1], col=to * 2 + k))
    yield
    for copy in first:
        copy.wait_recv()
    r2[x, 0:n] = (part[k * 4 + z] + r1[0]) + (r1[1] + r1[2])
    if key is not None:
        r2[x, n:] = (key[...] + kbuf[0]) + (kbuf[1] + kbuf[2])
    second = [net.send(r2.at[x], r2.at[x], row=y * 4 + (x + j) % 4) for j in range(1, 4)]
    yield
    for copy in second:
        copy.wait_recv()
    r3[y] = (r2[0] + r2[1]) + (r2[2] + r2[3])
    third = [net.send(r3.at[y], r3.at[y], row=(y + j) % 4 * 4 + x) for j in range(1, 4)]
    yield
    for copy in third:
        copy.wait_recv()
    at = k * 4 + z
    full[at] = (r3[0, 0:n] + r3[1, 0:n]) + (r3[2, 0:n] + r3[3, 0:n])
    fourth = [net.send(full.at[at], full.at[at], col=(z + j) % 4 * 2 + k) for j in range(1, 4)]
    yield
    for copy in fourth:
        copy.wait_recv()
    net.send(full.at[mine], full.at[mine], col=sibling).wait_recv()


def key_total(r3, n):
    return (r3[0, n:] + r3[1, n:]) + (r3[2, n:] + r3[3, n:])


def reduce_scratch(n, extra):
    return [
        pltpu.VMEM((8, n, D), F32),
        pltpu.VMEM((8, D), F32),
        pltpu.VMEM((4, n, D), F32),
        pltpu.VMEM((3, n, D), F32),
        pltpu.VMEM((5, 8, D), F32),
        pltpu.VMEM((4, n + extra, D), F32),
        pltpu.VMEM((4, n + extra, D), F32),
        pltpu.VMEM((8, n, D), F32),
    ]


REDUCE_COPIES = 2 + 6 + 3 + 3 + 3 + 1


def row_order(net, base):
    if base == 0:
        return net.x, net.y, lambda first, then: then % 4 * 4 + first % 4
    return net.y, net.x, lambda first, then: first % 4 * 4 + then % 4


def gather_half(net, mine, panel, base, done, keep):
    a, b, slot = row_order(net, base)
    all_rows, up, down = pl.ds(base, HALF), pl.ds(base, QUART), pl.ds(base + QUART, QUART)

    def pair(src, at, rows, plus, minus):
        view = panel.at[at, rows]
        source = view if src is None else src.at[rows]
        return net.send(source, view, row=plus), net.send(source, view, row=minus)

    def forward(at, rows, row):
        return net.send(panel.at[at, rows], panel.at[at, rows], row=row)

    own = slot(a, b)
    a_plus, a_minus = slot(a + 1, b), slot(a - 1 + 4, b)
    b_plus, b_minus = slot(a, b + 1), slot(a, b - 1 + 4)
    from_left, from_right = pair(mine, own, all_rows, a_plus, a_minus)
    yield
    second = {0: pair(mine, own, all_rows, b_plus, b_minus)}
    yield
    from_left.wait_recv()
    fwd_up = forward(slot(a + 3, b), up, a_plus)
    second[3] = pair(None, slot(a + 3, b), all_rows, b_plus, b_minus)
    from_right.wait_recv()
    fwd_down = forward(slot(a + 1, b), down, a_minus)
    yield
    second[1] = pair(None, slot(a + 1, b), all_rows, b_plus, b_minus)
    done(3, 0)
    done(1, 0)

    def pass_on(o):
        left, right = second[o]
        left.wait_recv()
        keep(0, o, panel.at[slot(a + o, b + 3), up])
        right.wait_recv()
        keep(1, o, panel.at[slot(a + o, b + 1), down])
        done(o, 3)
        done(o, 1)

    yield
    pass_on(0)
    yield
    fwd_up.wait_recv()
    fwd_down.wait_recv()
    second[2] = pair(None, slot(a + 2, b), all_rows, b_plus, b_minus)
    done(2, 0)
    yield
    pass_on(3)
    yield
    pass_on(1)
    yield
    pass_on(2)


GATHER_COPIES = 2 + 2 + 4 * 2


def gather_cols(net, mine, panel, done):
    z, k = net.z, net.k
    own = net.c
    plus, minus = (z + 1) % 4 * 2 + k, (z + 3) % 4 * 2 + k
    opposite = (z + 2) % 4 * 2 + k
    sibling = z * 2 + 1 - k
    up, down = pl.ds(0, HALF), pl.ds(HALF, HALF)
    left = net.send(mine, panel.at[own], col=plus)
    right = net.send(mine, panel.at[own], col=minus)
    pair = [net.send(mine, panel.at[own], col=sibling)]
    yield
    left.wait_recv()
    f_up = net.send(panel.at[minus, up], panel.at[minus, up], col=plus)
    pair.append(net.send(panel.at[minus], panel.at[minus], col=sibling))
    right.wait_recv()
    f_down = net.send(panel.at[plus, down], panel.at[plus, down], col=minus)
    pair.append(net.send(panel.at[plus], panel.at[plus], col=sibling))
    done(minus)
    done(plus)
    yield
    f_up.wait_recv()
    f_down.wait_recv()
    pair.append(net.send(panel.at[opposite], panel.at[opposite], col=sibling))
    done(opposite)
    yield
    for o, copy in zip((0, 3, 1, 2), pair):
        copy.wait_recv()
        done((z + o) % 4 * 2 + 1 - k)
    yield


COLS_COPIES = 3 + 4 + 1


def drive(order, **runs):
    def step(name):
        try:
            next(runs[name])
        except StopIteration:
            del runs[name]

    for name in order:
        if name in runs:
            step(name)
    while runs:
        for name in list(runs):
            step(name)


GATHER_ORDER = "abtctabotabtabtctbtaababctabctabtab"


def gather_kernel(
    x_ref, c_ref, wq_ref, wk_ref, wv_ref,
    xs_ref, cs_ref, last0, last1, last2, last3, att_out, gq_out, key_out, val_out, gs_ref, gks_ref,
    att_ref, gq_ref, key_ref, val_ref, q_ref, xp, cp, x_stage, c_stage, stage_sem, ssem, rsem, *reduce_refs,
):
    net = Net(ssem, rsem)
    net.barrier()
    last_refs = (last0, last1, last2, last3)
    ar1, ar2 = reduce_refs[:8], reduce_refs[8:]
    staged = []

    def send_out(source, target):
        copy = pltpu.make_async_copy(source, target, stage_sem.at[len(staged)])
        copy.start()
        staged.append(copy)

    def split_out(source, stage, out, slot, first=0, blocks=BLK):
        @pl.loop(first, first + blocks)
        def _(i):
            hi, lo = split2(source[pl.ds(pl.multiple_of(i * TILE, TILE), TILE), :])
            stage[slot, i, 0:TILE, :] = hi
            stage[slot, i, TILE : 2 * TILE, :] = lo

        at = pl.ds(first, blocks)
        send_out(stage.at[slot, at], out.at[slot, at])

    def x_done(half, dx, dy):
        slot = (net.y + dy) % 4 * 4 + (net.x + dx) % 4
        split_out(xp.at[slot], x_stage, xs_ref, slot, half * BLK // 2, BLK // 2)

    def keep(half):
        return lambda way, o, source: send_out(source, last_refs[2 * half + way].at[o])

    def cols_done(slot):
        split_out(cp.at[slot], c_stage, cs_ref, slot)

    def attention():
        def first(i, sums):
            state, key_sum = sums
            rows = pl.ds(pl.multiple_of(i * CH, CH), CH)
            x = x_ref[rows, :]
            q_ref[rows, :] = dot(x, wq_ref[...])
            key = dot(x, wk_ref[...])
            val = dot(x, wv_ref[...])
            key_ref[rows, :] = key
            val_ref[rows, :] = val
            feat_k = feat(key)
            return state + dot(feat_k, val, TN), key_sum + jnp.sum(feat_k, axis=0, keepdims=True)

        zero = (jnp.zeros((D, D), F32), jnp.zeros((1, D), F32))
        state, key_sum = lax.fori_loop(0, NODE // CH, first, zero)
        send_out(key_ref, key_out)
        send_out(val_ref, val_out)
        ar1[0][...] = state.reshape(8, 32, D)
        ar1[1][...] = jnp.broadcast_to(key_sum, (8, D))
        yield from all_reduce(net, *ar1)
        state = ar1[7][...].reshape(D, D)
        key_row = key_total(ar1[6], 32)[0:1]

        def second(i, sums):
            grad_state, grad_key_sum = sums
            rows = pl.ds(pl.multiple_of(i * CH, CH), CH)
            q = q_ref[rows, :]
            cot = c_ref[rows, :]
            feat_q = feat(q)
            den = jnp.sum(feat_q * key_row, axis=1, keepdims=True)
            att = dot(feat_q, state) / den
            att_ref[rows, :] = att
            scaled = cot / den
            weight_dot = jnp.sum(cot * att, axis=1, keepdims=True) / den
            gq_ref[rows, :] = (dot(scaled, state, NT) - weight_dot * key_row) * slope(q)
            return (
                grad_state + dot(feat_q, scaled, TN),
                grad_key_sum - jnp.sum(feat_q * weight_dot, axis=0, keepdims=True),
            )

        grad_state, grad_key_sum = lax.fori_loop(0, NODE // CH, second, zero)
        send_out(att_ref, att_out)
        send_out(gq_ref, gq_out)
        ar2[0][...] = grad_state.reshape(8, 32, D)
        ar2[1][...] = jnp.broadcast_to(grad_key_sum, (8, D))
        yield from all_reduce(net, *ar2)
        gs_ref[...] = ar2[7][...].reshape(D, D)
        gks_ref[...] = key_total(ar2[6], 32)

    def own_blocks():
        yield
        split_out(x_ref, x_stage, xs_ref, net.r)
        split_out(c_ref, c_stage, cs_ref, net.c)

    drive(
        GATHER_ORDER,
        a=gather_half(net, x_ref, xp, 0, lambda dx, dy: x_done(0, dx, dy), keep(0)),
        b=gather_half(net, x_ref, xp, HALF, lambda dy, dx: x_done(1, dx, dy), keep(1)),
        c=gather_cols(net, c_ref, cp, cols_done),
        t=attention(),
        o=own_blocks(),
    )
    net.finish()
    for copy in staged:
        copy.wait()


def run_gather(x, cot, wq, wk, wv):
    copies = 2 * GATHER_COPIES + COLS_COPIES + 2 * REDUCE_COPIES
    block = jax.ShapeDtypeStruct((NODE, D), F32)
    vmem, hbm = pl.BlockSpec(memory_space=pltpu.VMEM), pl.BlockSpec(memory_space=pl.ANY)
    return pl.pallas_call(
        gather_kernel,
        out_shape=[
            jax.ShapeDtypeStruct((16, BLK, 2 * TILE, D), BF16),
            jax.ShapeDtypeStruct((8, BLK, 2 * TILE, D), BF16),
            *[jax.ShapeDtypeStruct((4, QUART, D), F32)] * 4,
            block, block, block, block,
            jax.ShapeDtypeStruct((D, D), F32),
            jax.ShapeDtypeStruct((8, D), F32),
        ],
        in_specs=[vmem] * 5,
        out_specs=[hbm] * 10 + [vmem] * 2,
        scratch_shapes=[
            *[pltpu.VMEM((NODE, D), F32)] * 5,
            pltpu.VMEM((16, NODE, D), F32),
            pltpu.VMEM((8, NODE, D), F32),
            pltpu.VMEM((16, BLK, 2 * TILE, D), BF16),
            pltpu.VMEM((8, BLK, 2 * TILE, D), BF16),
            pltpu.SemaphoreType.DMA((2 * 11 + 16 + 9 + 4,)),
            pltpu.SemaphoreType.DMA((copies,)),
            pltpu.SemaphoreType.DMA((copies,)),
        ]
        + reduce_scratch(32, 8)
        + reduce_scratch(32, 8),
        compiler_params=pltpu.CompilerParams(
            collective_id=0, has_side_effects=True, vmem_limit_bytes=60 * 2**20
        ),
        name="gather",
    )(x, cot, wq, wk, wv)


CHUNK = 48
SLOTS = 3


def fetch(chunk, slot, tiles_ref, buf, tile_sem):
    return pltpu.make_async_copy(
        tiles_ref.at[pl.ds(chunk * CHUNK, CHUNK)], buf.at[slot], tile_sem.at[slot]
    )


def first_tiles(count, *refs):
    for i in range(SLOTS - 1):
        @pl.when(i * CHUNK < count)
        def _(i=i):
            fetch(i, i, *refs).start()


def sweep(count, rows_ref, cols_ref, tiles_ref, buf, tile_sem, body):
    chunks = (count + CHUNK - 1) // CHUNK
    refs = (tiles_ref, buf, tile_sem)

    @pl.loop(0, chunks)
    def _(chunk):
        slot = chunk % SLOTS

        @pl.when(chunk + SLOTS - 1 < chunks)
        def _():
            fetch(chunk + SLOTS - 1, (chunk + SLOTS - 1) % SLOTS, *refs).start()

        fetch(chunk, slot, *refs).wait()
        for i in range(CHUNK):
            at = chunk * CHUNK + i
            tile = buf[slot, i]
            body(jnp.where(at < count, tile, 0.0), rows_ref[at], cols_ref[at])


def product(tile, panel):
    hi, lo = split2(tile)
    whole = jnp.dot(jnp.concatenate([hi, hi], axis=1), panel, preferred_element_type=F32)
    return whole + jnp.dot(lo, panel[0:TILE], preferred_element_type=F32)


def block_rows(block):
    return pl.ds(pl.multiple_of(block * TILE, TILE), TILE)


def backward_kernel(
    rows_ref, cols_ref, count_ref, place_ref, tiles_ref, cs_ref,
    t_ref, leaf0, leaf1, leaf2, leaf3,
    cs, t, buf, sem, tile_sem,
):
    load = pltpu.make_async_copy(cs_ref, cs, sem.at[0])
    first_tiles(count_ref[0], tiles_ref, buf, tile_sem)
    load.start()
    t[...] = jnp.zeros_like(t)
    load.wait()

    def body(tile, row, col):
        t[block_rows(col), :] += product(tile.T, cs[row])

    sweep(count_ref[0], rows_ref, cols_ref, tiles_ref, buf, tile_sem, body)
    y, x = place_ref[0], place_ref[1]
    stores = [pltpu.make_async_copy(t, t_ref, sem.at[0])]
    for kind, leaf in enumerate((leaf0, leaf1, leaf2, leaf3)):
        for i, o in enumerate(SCATTER_TURNS):
            dx, dy = (o, 2) if kind < 2 else (2, o)
            slot = (y + dy) % 4 * 4 + (x + dx) % 4
            source = t.at[pl.ds(pl.multiple_of(slot * NODE + kind * QUART, QUART), QUART)]
            stores.append(pltpu.make_async_copy(source, leaf.at[i], sem.at[1 + 4 * kind + i]))
    for copy in stores:
        copy.start()
    for copy in stores:
        copy.wait()


def forward_kernel(
    rows_ref, cols_ref, count_ref, place_ref, tiles_ref, xs_ref, last0, last1, last2, last3,
    f_ref,
    xs, f, late, buf, sem, tile_sem,
):
    load = pltpu.make_async_copy(xs_ref, xs, sem.at[0])
    loads = [
        pltpu.make_async_copy(last, late.at[kind], sem.at[1 + kind])
        for kind, last in enumerate((last0, last1, last2, last3))
    ]
    first_tiles(count_ref[0], tiles_ref, buf, tile_sem)
    for copy in loads + [load]:
        copy.start()
    f[...] = jnp.zeros_like(f)
    for copy in loads + [load]:
        copy.wait()
    y, x = place_ref[0], place_ref[1]
    for kind in range(4):
        for o in range(4):
            dx, dy = (o, 2) if kind < 2 else (2, o)
            slot = (y + dy) % 4 * 4 + (x + dx) % 4
            for part in range(0, QUART, PART):
                block, at = divmod(kind * QUART + part, TILE)
                hi, lo = split2(late[kind, o, part : part + PART, :])
                xs[slot * BLK + block, at : at + PART, :] = hi
                xs[slot * BLK + block, TILE + at : TILE + at + PART, :] = lo

    def body(tile, row, col):
        f[block_rows(row), :] += product(tile, xs[col])

    sweep(count_ref[0], rows_ref, cols_ref, tiles_ref, buf, tile_sem, body)
    store = pltpu.make_async_copy(f, f_ref, sem.at[0])
    store.start()
    store.wait()


PART = 64
SCATTER_TURNS = (2, 1, 3, 0)


def run_sweep(kernel, name, out_shape, scratch, sems, scalars, tiles, *panels):
    hbm, smem = pl.BlockSpec(memory_space=pltpu.HBM), pl.BlockSpec(memory_space=pltpu.SMEM)
    return pl.pallas_call(
        kernel,
        out_shape=out_shape,
        in_specs=[smem] * 4 + [hbm] * (1 + len(panels)),
        out_specs=[hbm] * len(out_shape),
        scratch_shapes=scratch
        + [
            pltpu.VMEM((SLOTS, CHUNK, TILE, TILE), F32),
            pltpu.SemaphoreType.DMA((sems,)),
            pltpu.SemaphoreType.DMA((SLOTS,)),
        ],
        cost_estimate=pl.CostEstimate(
            flops=12 * MAXT * TILE * TILE * D, bytes_accessed=60 * 2**20, transcendentals=0
        ),
        compiler_params=pltpu.CompilerParams(vmem_limit_bytes=63 * 2**20),
        name=name,
    )(*scalars, tiles, *panels)


def run_backward(scalars, tiles, cs):
    leaf = jax.ShapeDtypeStruct((4, QUART, D), F32)
    return run_sweep(
        backward_kernel, "backward",
        [jax.ShapeDtypeStruct((16 * NODE, D), F32)] + [leaf] * 4,
        [pltpu.VMEM((8 * BLK, 2 * TILE, D), BF16), pltpu.VMEM((16 * NODE, D), F32)],
        17, scalars, tiles, cs.reshape(8 * BLK, 2 * TILE, D),
    )


def run_forward(scalars, tiles, xs, late):
    return run_sweep(
        forward_kernel, "forward",
        [jax.ShapeDtypeStruct((8 * NODE, D), F32)],
        [
            pltpu.VMEM((16 * BLK, 2 * TILE, D), BF16),
            pltpu.VMEM((8 * NODE, D), F32),
            pltpu.VMEM((4, 4, QUART, D), F32),
        ],
        5, scalars, tiles, xs.reshape(16 * BLK, 2 * TILE, D), *late,
    )[0]


def ring_sends(arrays):
    ways = ((1, 0), (3, 0), (0, 1), (0, 3))
    sent = []
    for array, (dy, dx) in zip(arrays, ways):
        pairs = [(y * 4 + x, (y + dy) % 4 * 4 + (x + dx) % 4) for y in range(4) for x in range(4)]
        sent.append(lax.ppermute(array, "rows", pairs))
    return sent


def scatter_half(net, t, base, leaf, main, leaf2, main2, own_ref, need):
    s, b, slot = row_order(net, base)
    up, down, both = pl.ds(base, QUART), pl.ds(base + QUART, QUART), pl.ds(base, HALF)
    order = SCATTER_TURNS
    b_plus, b_minus = slot(s, b + 1), slot(s, b + 3)
    mains = []
    s_plus, s_minus = slot(s + 1, b), slot(s + 3, b)

    def main_sends(i):
        o = order[i]
        plus, minus = slot(s + o, b + 1), slot(s + o, b + 3)
        need(o, 1)
        need(o, 3)
        t[plus, up] += leaf[0, i]
        t[minus, down] += leaf[1, i]
        return (
            net.send(t.at[plus, both], main.at[i, 0], row=b_plus),
            net.send(t.at[minus, both], main.at[i, 1], row=b_minus),
        )

    def collect(i):
        for copy in mains[i]:
            copy.wait_recv()
        at = slot(s + order[i], b)
        need(order[i], 0)
        t[at, both] += main[i, 0] + main[i, 1]
        return at

    mains.append(main_sends(0))
    yield
    mains.append(main_sends(1))
    yield
    mains.append(main_sends(2))
    yield
    at = collect(0)
    leaves2 = (
        net.send(t.at[at, up], leaf2.at[0], row=s_plus),
        net.send(t.at[at, down], leaf2.at[1], row=s_minus),
    )
    yield
    mains.append(main_sends(3))
    yield
    collect(1)
    yield
    collect(2)
    for copy in leaves2:
        copy.wait_recv()
    t[s_plus, up] += leaf2[0]
    t[s_minus, down] += leaf2[1]
    mains2 = (
        net.send(t.at[s_plus, both], main2.at[0], row=s_plus),
        net.send(t.at[s_minus, both], main2.at[1], row=s_minus),
    )
    yield
    collect(3)
    yield
    for copy in mains2:
        copy.wait_recv()
    own_ref[both, :] = t[slot(s, b), both] + (main2[0] + main2[1])


SCATTER_COPIES = 4 * 2 + 2 + 2


def scatter_cols(net, f_hbm, f, pair, leaf, main, ready):
    z, k = net.z, net.k
    up, down = pl.ds(0, HALF), pl.ds(HALF, HALF)
    order = (2, 1, 3, 0)
    copies = [
        net.send(f_hbm.at[(z + o) % 4 * 2 + 1 - k], pair.at[i], col=z * 2 + 1 - k)
        for i, o in enumerate(order)
    ]
    yield
    plus, minus = (z + 1) % 4 * 2 + k, (z + 3) % 4 * 2 + k
    for i, o in enumerate(order):
        copies[i].wait_recv()
        ready(o)
        at = (z + o) % 4 * 2 + k
        f[at] += pair[i]
        if o == 2:
            leaves = (
                net.send(f.at[at, up], leaf.at[0], col=plus),
                net.send(f.at[at, down], leaf.at[1], col=minus),
            )
            yield
    yield
    for copy in leaves:
        copy.wait_recv()
    f[plus, up] += leaf[0]
    f[minus, down] += leaf[1]
    mains = (
        net.send(f.at[plus], main.at[0], col=plus),
        net.send(f.at[minus], main.at[1], col=minus),
    )
    yield
    for copy in mains:
        copy.wait_recv()
    f[net.c] += main[0] + main[1]


SCATTER_COLS_COPIES = 4 + 2 + 2


SCATTER_ORDER = "gabgabtgabttgabtabgtabgabtgabgtg"


T_ORDER = [(2, 1), (2, 3), (1, 2), (3, 2), (1, 1), (1, 3), (3, 1), (3, 3), (2, 0), (0, 2)]
T_ORDER += [(0, 1), (0, 3), (1, 0), (3, 0), (0, 0), (2, 2)]


def scatter_kernel(
    x_in, c_in, wq_ref, wk_ref, wv_ref, wg_ref,
    att_in, gq_in, key_in, val_in, gs_ref, gks_ref, f_hbm, t_hbm, first0, first1, first2, first3,
    own_ref, out_hbm, gx_hbm, dq_ref, dk_ref, dv_ref, dg_ref,
    x_ref, c_ref, att_ref, gq_ref, key_ref, val_ref, out_ref, gx_ref, store_sem,
    f, t, leaf, main, leaf2, main2, pair, zleaf, zmain, load_sem, ssem, rsem, *reduce_refs,
):
    net = Net(ssem, rsem)
    loads = {}

    def load(key, source, target):
        loads[key] = pltpu.make_async_copy(source, target, load_sem.at[len(loads)])
        loads[key].start()

    for i, first in enumerate((first0, first1, first2, first3)):
        load(i, first, leaf.at[i // 2, i % 2])
    for i, (dx, dy) in enumerate(T_ORDER):
        slot = (net.y + dy) % 4 * 4 + (net.x + dx) % 4
        load((dx, dy), t_hbm.at[slot], t.at[slot])
        if i == 3:
            for o in (2, 1, 3, 0):
                at = (net.z + o) % 4 * 2 + net.k
                load(("f", o), f_hbm.at[at], f.at[at])
            load("gq", gq_in, gq_ref)
            load("key", key_in, key_ref)
            load("val", val_in, val_ref)
            load("x", x_in, x_ref)
    load("cot", c_in, c_ref)
    load("att", att_in, att_ref)
    stores = [
        pltpu.make_async_copy(gx_ref, gx_hbm, store_sem.at[0]),
        pltpu.make_async_copy(out_ref, out_hbm, store_sem.at[1]),
    ]
    net.barrier()
    ar1, ar2 = reduce_refs[:8], reduce_refs[8:]

    def need(*keys):
        for key in keys:
            if key in loads:
                loads.pop(key).wait()

    def attention():
        need("gq", "key", "val", "x")
        for i in range(NODE // CH):
            rows = pl.ds(i * CH, CH)
            x = x_ref[rows, :]
            key = key_ref[rows, :]
            gq = gq_ref[rows, :]
            gk = (dot(val_ref[rows, :], gs_ref[...], NT) + gks_ref[0:1, :]) * slope(key)
            gv = dot(feat(key), gs_ref[...])
            gx = dot(gq, wq_ref[...], NT) + dot(gk, wk_ref[...], NT)
            gx_ref[rows, :] = gx + dot(gv, wv_ref[...], NT)
            for j, grad in enumerate((gq, gk, gv)):
                product = dot(x, grad, TN).reshape(8, 32, D)
                at = pl.ds(32 * j, 32)
                ar1[0][:, at, :] = product if i == 0 else ar1[0][:, at, :] + product
            yield
        stores[0].start()
        yield from all_reduce(net, ar1[0], None, *ar1[2:])
        for j, grad in enumerate((dq_ref, dk_ref, dv_ref)):
            grad[...] = ar1[7][:, pl.ds(32 * j, 32), :].reshape(D, D)

    def graph():
        yield from scatter_cols(net, f_hbm, f, pair, zleaf, zmain, lambda o: need(("f", o)))
        dg_ref[...] = jnp.zeros((D, D), F32)
        need("cot", "att")

        @pl.loop(0, NODE // CH)
        def _(i):
            rows = pl.ds(pl.multiple_of(i * CH, CH), CH)
            mixed = f[net.c, rows, :]
            out_ref[rows, :] = att_ref[rows, :] + dot(mixed, wg_ref[...])
            dg_ref[...] += dot(mixed, c_ref[rows, :], TN)

        stores[1].start()
        ar2[0][...] = dg_ref[...].reshape(8, 32, D)
        yield from all_reduce(net, ar2[0], None, *ar2[2:])
        dg_ref[...] = ar2[7][...].reshape(D, D)

    def half(i):
        def wanted(small, big):
            need(0, 1, 2, 3, (small, big) if i == 0 else (big, small))

        return scatter_half(net, t, i * HALF, leaf.at[i], main.at[i], leaf2.at[i], main2.at[i], own_ref, wanted)

    drive(SCATTER_ORDER, a=half(0), b=half(1), g=graph(), t=attention())
    need(*list(loads))
    for copy in stores:
        copy.wait()
    net.finish()


def run_scatter(x, cot, wq, wk, wv, wg, att, gq, key, val, gs, gks, f, t, firsts):
    copies = 2 * SCATTER_COPIES + SCATTER_COLS_COPIES + 2 * REDUCE_COPIES
    block, weight = jax.ShapeDtypeStruct((NODE, D), F32), jax.ShapeDtypeStruct((D, D), F32)
    vmem, hbm = pl.BlockSpec(memory_space=pltpu.VMEM), pl.BlockSpec(memory_space=pltpu.HBM)
    return pl.pallas_call(
        scatter_kernel,
        out_shape=[block, block, block, weight, weight, weight, weight],
        in_specs=[hbm] * 2 + [vmem] * 4 + [hbm] * 4 + [vmem] * 2 + [hbm] * 6,
        out_specs=[vmem] + [hbm] * 2 + [vmem] * 4,
        scratch_shapes=[
            *[pltpu.VMEM((NODE, D), F32)] * 8,
            pltpu.SemaphoreType.DMA((2,)),
            pltpu.VMEM((8, NODE, D), F32),
            pltpu.VMEM((16, NODE, D), F32),
            pltpu.VMEM((2, 2, 4, QUART, D), F32),
            pltpu.VMEM((2, 4, 2, HALF, D), F32),
            pltpu.VMEM((2, 2, QUART, D), F32),
            pltpu.VMEM((2, 2, HALF, D), F32),
            pltpu.VMEM((4, NODE, D), F32),
            pltpu.VMEM((2, HALF, D), F32),
            pltpu.VMEM((2, NODE, D), F32),
            pltpu.SemaphoreType.DMA((30,)),
            pltpu.SemaphoreType.DMA((copies,)),
            pltpu.SemaphoreType.DMA((copies,)),
        ]
        + reduce_scratch(96, 0)
        + reduce_scratch(32, 0),
        compiler_params=pltpu.CompilerParams(
            collective_id=1, has_side_effects=True, vmem_limit_bytes=60 * 2**20
        ),
        name="scatter",
    )(x, cot, wq, wk, wv, wg, att, gq, key, val, gs, gks, f, t, *firsts)


def finish_kernel(own_hbm, wg_ref, *refs):
    taken, given, held, (own, load_sem, store_sem) = refs[:6], refs[6:12], refs[12:18], refs[18:]
    loads = [pltpu.make_async_copy(own_hbm, own, load_sem.at[6])]
    for i in range(6):
        loads.append(pltpu.make_async_copy(taken[i], held[i], load_sem.at[i]))
    for copy in loads:
        copy.start()
    stores = [pltpu.make_async_copy(held[i], given[i], store_sem.at[i]) for i in range(6)]
    loads[0].wait()
    term = dot(own[...], wg_ref[...], NT)
    loads[1].wait()
    held[0][...] += term
    stores[0].start()
    for i in range(1, 6):
        loads[i + 1].wait()
        stores[i].start()
    for copy in stores:
        copy.wait()


def run_finish(own, wg, out, gx, *weights):
    vmem, hbm = pl.BlockSpec(memory_space=pltpu.VMEM), pl.BlockSpec(memory_space=pl.ANY)
    gx, out, *weights = pl.pallas_call(
        finish_kernel,
        out_shape=[jax.ShapeDtypeStruct(a.shape, F32) for a in (gx, out, *weights)],
        in_specs=[hbm, vmem] + [hbm] * 6,
        out_specs=[hbm] * 6,
        scratch_shapes=[
            *[pltpu.VMEM(a.shape, F32) for a in (gx, out, *weights)],
            pltpu.VMEM((NODE, D), F32),
            pltpu.SemaphoreType.DMA((7,)),
            pltpu.SemaphoreType.DMA((6,)),
        ],
        compiler_params=pltpu.CompilerParams(vmem_limit_bytes=60 * 2**20),
        name="finish",
    )(own, wg, gx, out, *weights)
    return (out, gx, *weights)


def per_device(x, cot, wq, wk, wv, wg, tiles, tile_rows, tile_cols, tile_count):
    xs, cs, *rest = run_gather(x, cot, wq, wk, wv)
    last, (att, gq, key, val, gs, gks) = rest[:4], rest[4:]
    row = lax.axis_index("rows")
    scalars = (tile_rows, tile_cols, tile_count, jnp.stack([row // 4, row % 4]))
    late = ring_sends(last)
    t, *leaves = run_backward(scalars, tiles, cs)
    firsts = ring_sends(leaves)
    f = run_forward(scalars, tiles, xs, late).reshape(8, NODE, D)
    t = t.reshape(16, NODE, D)
    own, *results = run_scatter(x, cot, wq, wk, wv, wg, att, gq, key, val, gs, gks, f, t, firsts)
    return run_finish(own, wg, *results)


def solution(mesh):
    nodes = P(("rows", "cols"), None)
    slots = P(("rows", "cols"))
    return jax.shard_map(
        per_device,
        mesh=mesh,
        in_specs=(nodes, nodes, P(), P(), P(), P(), P(("rows", "cols"), None, None), slots, slots, slots),
        out_specs=(nodes, nodes, P(), P(), P(), P()),
        check_vma=False,
    )
```
